32 devices in a mesh: dp: 8 (over z, y), section: 4 (over x, core).
Axes of the slice: x: 2, y: 2, z: 4, core: 2. Of those that a mesh axis runs over, the one named last changes fastest.
Arguments:
- tokens: bfloat16 [16384, 768], P('dp'), may hold values from -6 to 6
- cotangent: bfloat16 [16384, 768], P('dp'), may hold values from -6 to 6
- segment_ids: int32 [64, 256], P('dp'), may hold values from 0 to 7, never falling along the last dimension, each value on 1 to 128 neighbouring positions
- first_weight: bfloat16 [4, 768, 3072], P('section')
- down_weight: bfloat16 [4, 768, 3072], P('section'), may hold values from -0.109375 to 0.109375
- ln_gain: float32 [4, 768], P('section'), may hold values from 0.5 to 1.5
- ln_shift: float32 [4, 768], P('section'), may hold values from -3 to 3
Outputs:
- layer_output: bfloat16 [16384, 768], P(('dp', 'section'))
- input_grad: bfloat16 [16384, 768], P(('dp', 'section'))
- first_grad: float32 [4, 768, 3072], P('section', None, 'dp')
- down_grad: float32 [4, 768, 3072], P('section', None, 'dp')
- gain_grad: float32 [4, 768], P('section', 'dp')
- shift_grad: float32 [4, 768], P('section', 'dp')
The draws below stay inside these ranges and needn't reach their ends.
Inputs may be any that keep to these rules, and one draw needn't show every extreme that they name: `segment_ids`: along each row of 256 positions the numbers never fall; rows with equal numbers in one packed sequence form one document.
All inputs are finite; a program needn't handle non-finite values.
Results may differ from the reference program's by a relative error of at most 0.022.
Values may be sent and summed in bfloat16 or wider, within the bound.
A program may use at most 192 MiB of HBM per device.

```python
import math
import jax
import jax.numpy as jnp
import numpy as np
from jax import lax

D = 768
HEADS = 12
FF = 3072
SEQ = 256
TOKENS = 16384
NSEQ = 64
N_DP = 8
N_SECTION = 4


def draw_first_weight(key, part):
    key = jax.random.fold_in(key, 11)
    normal_draw = jnp.clip(jax.random.normal(key, (N_SECTION, D, FF), jnp.float32), -6.0, 6.0) * D ** (-0.5)
    section_rows = jnp.arange(N_SECTION)[:, None, None]
    column = jnp.arange(FF)[None, None, :]
    column_boost = jnp.where((section_rows % 2 == 0) & (column >= 3 * D), 4.0, 1.0)
    return (normal_draw * column_boost).astype(jnp.bfloat16)


def levels(stream_key, shape, pieces, smallest, largest):
    level, own = 1.0, jax.random.fold_in(stream_key, 6)
    for axis_at, shards_of in pieces:
        heights = jnp.exp(jax.random.uniform(jax.random.fold_in(own, axis_at), (shards_of,), jnp.float32, smallest / len(pieces), largest / len(pieces)))
        level = level * jnp.repeat(heights, shape[axis_at] // shards_of).reshape([-1 if axis == axis_at else 1 for axis in range(len(shape))])
    return level


def split_up(count, total, limit, slope):
    loads = [(1 << 20) // math.isqrt(standing ** slope) + 1 for standing in range(2, count + 1)]
    surplus, holding = total - limit - (count - 1), [1] * (count - 1)
    while surplus > 0:
        movable = [i for i in range(count - 1) if holding[i] < limit]
        pool, remaining = sum([loads[i] for i in movable]), surplus
        for i in movable:
            addition = min(limit - holding[i], max(1, remaining * loads[i] // pool), surplus)
            holding[i] = holding[i] + addition
            surplus = surplus - addition
    return np.array([limit] + holding)


def uneven(stream_key, count, total, reach, lean):
    if count == 2:
        one = jax.random.randint(stream_key, (), max(1, total - reach), min(reach, total - 1) + 1)
        return jnp.stack([one, total - one])
    sizes = jnp.asarray(split_up(count, total, reach, lean), jnp.int32)
    pairs = (count - 1) // 2
    source_of, taker = sizes[1:1 + 2 * pairs:2], sizes[2:2 + 2 * pairs:2]
    margin = jnp.minimum(source_of - 1, reach - taker)
    moved = jax.random.randint(jax.random.fold_in(stream_key, 1), (pairs,), 0, 1 << 20) % (margin + 1)
    sizes = sizes.at[1:1 + 2 * pairs:2].set(source_of - moved).at[2:2 + 2 * pairs:2].set(taker + moved)
    return sizes[jax.random.permutation(jax.random.fold_in(stream_key, 2), count)]


def bell_draw(key, extent, scale, limit, shards=(), dtype=jnp.bfloat16):
    loudness = levels(key, extent, shards, -0.22, 0.18) if shards else 1.0
    entries = jax.random.normal(key, extent, jnp.float32) * scale * loudness
    return jnp.minimum(jnp.maximum(entries, -limit), limit).astype(dtype)


def setup_inputs(seed: int = 0) -> dict:
    streams_of = jax.random.split(jax.random.key(seed), 8)
    tokens = bell_draw(streams_of[0], (TOKENS, D), 1.0, 6.0, ((0, 8),))
    cotangent = bell_draw(streams_of[1], (TOKENS, D), 1.0, 6.0, ((0, 8),))
    segment_ids = jax.vmap(lambda own: jnp.searchsorted(jnp.cumsum(uneven(own, 8, SEQ, SEQ // 2, 2)), jnp.arange(SEQ), side="right"))(jax.random.split(streams_of[2], NSEQ)).reshape((NSEQ, SEQ)).astype(jnp.int32)
    first_weight = draw_first_weight(jax.random.fold_in(streams_of[7], 71), 0)
    down_weight = bell_draw(streams_of[4], (N_SECTION, D, FF), FF ** -0.5, 0.109375, ((0, 4),))
    ln_gain = jnp.clip(1.0 + 0.1 * jax.random.normal(streams_of[5], (N_SECTION, D), jnp.float32), 0.5, 1.5)
    ln_shift = bell_draw(streams_of[6], (N_SECTION, D), 0.5, 3.0, ((0, 4),), jnp.float32)
    return {"tokens": tokens, "cotangent": cotangent, "segment_ids": segment_ids, "first_weight": first_weight, "down_weight": down_weight, "ln_gain": ln_gain, "ln_shift": ln_shift}


@jax.custom_vjp
def low(v):
    return lax.optimization_barrier(v.astype(jnp.bfloat16)).astype(jnp.float32)

@jax.custom_vjp
def low_back(v):
    return v

def low_keep(v):
    return (low(v), None)

def low_pass(kept, grad):
    return (grad,)

def back_keep(v):
    return (v, None)

def back_low(kept, grad):
    return (low(grad),)
low.defvjp(low_keep, low_pass)
low_back.defvjp(back_keep, back_low)
NORM_EPSILON = 1e-12
MASKED_SCORE = -1e+30
PRECISE = lax.Precision.HIGHEST

def norm_rows(residual, gain_row, shift_row):
    row_mean = lax.optimization_barrier(jnp.mean(residual, axis=-1, keepdims=True))
    centered = residual - row_mean
    spread = lax.optimization_barrier(jnp.mean(centered * centered, axis=-1, keepdims=True))
    return centered * lax.rsqrt(spread + NORM_EPSILON) * gain_row + shift_row

def attend_block(inputs, weight, gain_row, shift_row, segment_rows):
    seq_count, seq_length, model_width = inputs.shape
    head_width = model_width // HEADS
    projected = jnp.einsum('bsd,de->bse', inputs, weight[:, :3 * model_width], precision=PRECISE)
    projected = low_back(low(projected)).reshape(seq_count, seq_length, 3, HEADS, head_width)
    queries = projected[:, :, 0]
    key_rows = projected[:, :, 1]
    values = projected[:, :, 2]
    scores = jnp.einsum('bqhd,bkhd->bhqk', queries, key_rows, precision=PRECISE) * head_width ** (-0.5)
    allowed = (segment_rows[:, :, None] == segment_rows[:, None, :])[:, None]
    scores = low_back(jnp.where(allowed, scores, MASKED_SCORE))
    softmax_probs = jax.nn.softmax(scores, axis=-1)
    context = jnp.einsum('bhqk,bkhd->bqhd', low(softmax_probs), values, precision=PRECISE)
    context = low_back(low(context.reshape(seq_count, seq_length, model_width)))
    branch = low_back(jnp.einsum('bsd,de->bse', context, weight[:, 3 * model_width:], precision=PRECISE))
    return norm_rows(inputs + branch, gain_row, shift_row)

def feed_block(inputs, weight, down_rows, gain_row, shift_row):
    pre_gelu = low_back(jnp.einsum('bsd,df->bsf', inputs, weight, precision=PRECISE))
    hidden = low(jax.nn.gelu(pre_gelu, approximate=False))
    branch = low_back(jnp.einsum('bsf,df->bsd', hidden, down_rows, precision=PRECISE))
    return norm_rows(inputs + branch, gain_row, shift_row)

def forward_block(inputs, first, down, gains, shifts, segment_rows):
    state_rows = inputs
    for position in range(N_SECTION):
        if position > 0:
            state_rows = low_back(low(state_rows))
        if position % 2 == 0:
            state_rows = attend_block(state_rows, first[position], gains[position], shifts[position], segment_rows)
        else:
            state_rows = feed_block(state_rows, first[position], down[position], gains[position], shifts[position])
    return state_rows

def reference(tokens, cotangent, segment_ids, first_weight, down_weight, ln_gain, ln_shift):
    model_width = tokens.shape[1]
    inputs = tokens.astype(jnp.float32).reshape(N_DP, -1, SEQ, model_width)
    upstream = cotangent.astype(jnp.float32).reshape(N_DP, -1, SEQ, model_width)
    segment_groups = segment_ids.reshape(N_DP, -1, SEQ)
    first = first_weight.astype(jnp.float32)
    down = down_weight.astype(jnp.float32)

    def one_group(totals, block_item):
        block_in, block_up, block_seg = block_item

        def forward(rows_in, first_in, down_in, gain_in, shift_in):
            return forward_block(rows_in, first_in, down_in, gain_in, shift_in, block_seg)
        result, pullback = jax.vjp(forward, block_in, first, down, ln_gain, ln_shift)
        d_rows, d_first, d_down, d_gain, d_shift = pullback(block_up)
        totals = (totals[0] + d_first, totals[1] + d_down, totals[2] + d_gain, totals[3] + d_shift)
        return (totals, (result.astype(jnp.bfloat16), d_rows.astype(jnp.bfloat16)))
    starting = (jnp.zeros_like(first), jnp.zeros_like(down), jnp.zeros_like(ln_gain), jnp.zeros_like(ln_shift))
    totals, (out_rows, grad_rows) = lax.scan(one_group, starting, (inputs, upstream, segment_groups))
    return (out_rows.reshape(-1, model_width), grad_rows.reshape(-1, model_width), totals[0], totals[1], totals[2], totals[3])
```

```python
import functools

import jax
import jax.numpy as jnp
from jax import lax
from jax.experimental import pallas as pl
from jax.experimental.pallas import tpu as pltpu
from jax.sharding import PartitionSpec as P

HEADS = 12
NORM_EPSILON = 1e-12
MASKED_SCORE = -1e30
INV_SQRT2 = 0.7071067811865476
INV_SQRT2PI = 0.3989422804014327
MESH = pl.DeviceIdType.MESH
bf16 = jnp.bfloat16
f32 = jnp.float32


def dot(a, b):
    return jnp.dot(a, b, preferred_element_type=f32)


def dot_nt(a, b):
    return lax.dot_general(a, b, (((1,), (1,)), ((), ())), preferred_element_type=f32)


def dot_tn(a, b):
    return lax.dot_general(a, b, (((0,), (0,)), ((), ())), preferred_element_type=f32)


def aligned(index, size):
    return pl.ds(pl.multiple_of(index * size, size), size)


def norm_forward(residual, rows, gain, shift, refs):
    mean = jnp.mean(residual, axis=-1, keepdims=True)
    centered = residual - mean
    spread = jnp.mean(centered * centered, axis=-1, keepdims=True)
    scale = lax.rsqrt(spread + NORM_EPSILON)
    normal = centered * scale
    refs.normal[rows, :] = normal.astype(bf16)
    refs.scale[rows, :] = scale
    refs.out[rows, :] = (normal * gain + shift).astype(bf16)


def norm_backward(rows, gain, refs):
    upstream = refs.grad[rows, :].astype(f32)
    normal = refs.normal[rows, :].astype(f32)
    scale = refs.scale[rows, :]
    count, width = upstream.shape
    refs.norm_sums[0] += jnp.sum((upstream * normal).reshape(count // 8, 8, width), axis=0)
    refs.norm_sums[1] += jnp.sum(upstream.reshape(count // 8, 8, width), axis=0)
    pulled = upstream * gain
    mean = jnp.mean(pulled, axis=-1, keepdims=True)
    along = jnp.mean(pulled * normal, axis=-1, keepdims=True)
    d_resid = scale * (pulled - mean - normal * along)
    refs.grad[rows, :] = d_resid.astype(bf16)
    return d_resid


def feed_forward(rows, gain, shift, refs):
    width, hidden = refs.weight.shape
    tile = width
    tiles = hidden // tile
    source = refs.rows_in[rows, :]
    residual = source.astype(f32)

    def up(t):
        return dot(source, refs.weight[:, t * tile : (t + 1) * tile])

    def down(value, t):
        return dot_nt(value, refs.down[:, t * tile : (t + 1) * tile])

    pre = up(0)
    held = None
    for t in range(tiles):
        following = up(t + 1) if t + 1 < tiles else None
        cdf = 0.5 + 0.5 * lax.erf(pre * INV_SQRT2)
        value = (pre * cdf).astype(bf16)
        slope = cdf + pre * (INV_SQRT2PI * jnp.exp(-0.5 * pre * pre))
        refs.keep[rows, t * tile : (t + 1) * tile] = value
        refs.wide[rows, t * tile : (t + 1) * tile] = slope.astype(bf16)
        if held is not None:
            residual = residual + down(held, t - 1)
        held, pre = value, following
    residual = residual + down(held, tiles - 1)
    norm_forward(residual, rows, gain, shift, refs)


def feed_backward(rows, gain, refs):
    width, hidden = refs.weight.shape
    tile = width
    tiles = hidden // tile
    d_resid = norm_backward(rows, gain, refs)
    d_branch = d_resid.astype(bf16)
    total = d_resid

    def up(t):
        return dot(d_branch, refs.down[:, t * tile : (t + 1) * tile])

    def down(value, t):
        return dot_nt(value, refs.weight[:, t * tile : (t + 1) * tile])

    d_hidden = up(0)
    held = None
    for t in range(tiles):
        following = up(t + 1) if t + 1 < tiles else None
        columns = slice(t * tile, (t + 1) * tile)
        d_pre = (d_hidden * refs.wide[rows, columns].astype(f32)).astype(bf16)
        refs.wide[rows, columns] = d_pre
        if held is not None:
            total = total + down(held, t - 1)
        held, d_hidden = d_pre, following
    total = total + down(held, tiles - 1)
    refs.d_in[rows, :] = total.astype(bf16)


def head_part(refs, first_row, length, blocks, which, n):
    head_width = refs.weight.shape[0] // HEADS
    per_block = length // head_width
    column = (which * blocks + n // per_block) * length
    rows = pl.ds(pl.multiple_of(first_row + (n % per_block) * head_width, head_width), head_width)
    return rows, slice(column, column + length)


def attend_forward(index, gain, shift, refs):
    length = refs.segments.shape[1]
    width = refs.weight.shape[0]
    blocks = width // length
    rows = aligned(index, length)
    first_row = index * length
    source = refs.rows_in[rows, :]
    ids = jnp.broadcast_to(refs.segments[pl.ds(index, 1), :].astype(f32), (length, length))
    allowed = ids == ids.T
    score_scale = (width // HEADS) ** (-0.5)
    for which in range(3):
        turned = dot_nt(refs.down[:, which * width : (which + 1) * width], source)
        if which == 0:
            turned = turned * score_scale
        turned = turned.astype(bf16)
        for j in range(blocks):
            column = (which * blocks + j) * length
            refs.keep[rows, column : column + length] = turned[j * length : (j + 1) * length, :]
    place = functools.partial(head_part, refs, first_row, length, blocks)

    def score(n):
        return dot_tn(refs.keep[place(1, n)], refs.keep[place(0, n)])

    def weigh(scores):
        scores = jnp.where(allowed, scores, MASKED_SCORE)
        raw = jnp.exp(scores - jnp.max(scores, axis=0, keepdims=True))
        return raw.astype(bf16), 1.0 / jnp.sum(raw, axis=0, keepdims=True)

    def finish(n, raw, inverse):
        refs.wide[rows, n * length : (n + 1) * length] = raw
        refs.inverse[pl.ds(index * 16 + n, 1), :] = inverse
        refs.keep[place(3, n)] = (dot(refs.keep[place(2, n)], raw) * inverse).astype(bf16)

    ahead = 2
    scores = [score(n) for n in range(ahead)]
    held = None
    for n in range(HEADS):
        if n + ahead < HEADS:
            scores.append(score(n + ahead))
        current = weigh(scores[n])
        if held is not None:
            finish(n - 1, *held)
        held = current
    finish(HEADS - 1, *held)
    residual = source.astype(f32)
    for j in range(blocks):
        column = (3 * blocks + j) * length
        residual = residual + dot_tn(
            refs.keep[rows, column : column + length],
            refs.weight[j * length : (j + 1) * length, 3 * width :],
        )
    norm_forward(residual, rows, gain, shift, refs)


def attend_backward(index, gain, refs):
    length = refs.segments.shape[1]
    width = refs.weight.shape[0]
    head_width = width // HEADS
    blocks = width // length
    per_block = length // head_width
    score_scale = head_width ** (-0.5)
    rows = aligned(index, length)
    first_row = index * length
    d_resid = norm_backward(rows, gain, refs)
    refs.d_context[...] = dot_nt(refs.weight[:, 3 * width :], d_resid.astype(bf16))
    place = functools.partial(head_part, refs, first_row, length, blocks)

    def first(n):
        inverse = refs.inverse[pl.ds(index * 16 + n, 1), :]
        d_context = refs.d_context[n * head_width : (n + 1) * head_width, :] * inverse
        along = jnp.sum(d_context * refs.keep[place(3, n)].astype(f32), axis=0, keepdims=True)
        d_context = d_context.astype(bf16)
        return dot_tn(refs.keep[place(2, n)], d_context), along, d_context

    def second(n, d_probs, along, d_context):
        raw = refs.wide[rows, n * length : (n + 1) * length]
        return (raw.astype(f32) * (d_probs - along)).astype(bf16), raw, d_context

    made = ([], [], [])

    def third(n, d_scores, raw, d_context):
        made[0].append(dot(refs.keep[place(1, n)], d_scores) * score_scale)
        made[1].append(dot_nt(refs.keep[place(0, n)], d_scores))
        made[2].append(dot_nt(d_context, raw))
        if n % per_block == per_block - 1:
            block = n // per_block
            for which in range(3):
                column = (which * blocks + block) * length
                whole = jnp.concatenate(made[which], axis=0).astype(bf16)
                refs.keep[rows, column : column + length] = whole.T
                made[which].clear()
            column = (3 * blocks + block) * length
            refs.keep[rows, column : column + length] = refs.keep[rows, column : column + length].T

    current = first(0)
    held = None
    for n in range(HEADS):
        following = first(n + 1) if n + 1 < HEADS else None
        ready = second(n, *current)
        if held is not None:
            third(n - 1, *held)
        held, current = ready, following
    third(HEADS - 1, *held)
    d_in = d_resid + dot_nt(refs.keep[rows, : 3 * width], refs.weight[:, : 3 * width])
    refs.d_in[rows, :] = d_in.astype(bf16)


class Refs:
    def __init__(self, **named):
        self.__dict__.update(named)


def pipeline(
    sections,
    tokens,
    cotangent,
    segments,
    weight_in,
    down_in,
    gain_in,
    shift_in,
    layer_out,
    input_out,
    weight_sums,
    norm_out,
    rows_in,
    keep,
    wide,
    grad,
    normal,
    scale,
    out,
    d_in,
    weight,
    down,
    norm_sums,
    d_context,
    inverse,
    load_sem,
    first_sem,
    forward_send,
    forward_recv,
    backward_send,
    backward_recv,
    share_send,
    share_recv,
    store_sem,
):
    dp = lax.axis_index("dp")
    section = lax.axis_index("section")
    batches, length = segments.shape
    width, hidden = weight.shape
    share = batches // sections
    final = sections - 1
    refs = Refs(
        rows_in=rows_in, keep=keep, wide=wide, grad=grad, normal=normal, scale=scale, out=out, d_in=d_in,
        weight=weight, down=down, norm_sums=norm_sums, d_context=d_context, inverse=inverse, segments=segments,
    )
    is_attention = lax.rem(section, 2) == 0
    is_feed = lax.rem(section, 2) == 1

    def load_rows(source, target, i):
        rows = aligned(i, length)
        return pltpu.make_async_copy(source.at[rows, :], target.at[rows, :], first_sem.at[i])

    load_weight = pltpu.make_async_copy(weight_in.at[0], weight, load_sem.at[0])
    load_down = pltpu.make_async_copy(down_in.at[0], down, load_sem.at[1])
    load_weight.start()

    @pl.when(is_feed)
    def _():
        load_down.start()

    @pl.when(section == 0)
    def _():
        for i in range(batches):
            load_rows(tokens, rows_in, i).start()

    @pl.when(section == final)
    def _():
        for i in range(batches):
            load_rows(cotangent, grad, i).start()

    barrier = pltpu.get_barrier_semaphore()
    for other in range(1, sections):
        pl.semaphore_signal(
            barrier, inc=1, device_id=(dp, lax.rem(section + other, sections)), device_id_type=MESH
        )
    pl.semaphore_wait(barrier, sections - 1)

    norm_sums[...] = jnp.zeros_like(norm_sums)
    gain = gain_in[...]
    shift = shift_in[...]

    def forward_copy(i):
        rows = aligned(i, length)
        return pltpu.make_async_remote_copy(
            out.at[rows, :], rows_in.at[rows, :], forward_send.at[i], forward_recv.at[i],
            device_id=(dp, lax.rem(section + 1, sections)), device_id_type=MESH,
        )

    def backward_copy(i):
        rows = aligned(i, length)
        return pltpu.make_async_remote_copy(
            d_in.at[rows, :], grad.at[rows, :], backward_send.at[i], backward_recv.at[i],
            device_id=(dp, lax.rem(section + sections - 1, sections)), device_id_type=MESH,
        )

    def share_copy(source, target, i, away):
        owner = i // share
        remote = pltpu.make_async_remote_copy(
            source.at[aligned(i, length), :], target.at[aligned(lax.rem(i, share), length), :],
            share_send.at[away, i], share_recv.at[away, lax.rem(i, share)],
            device_id=(dp, owner), device_id_type=MESH,
        )
        local = pltpu.make_async_copy(
            source.at[aligned(i, length), :], target.at[aligned(lax.rem(i, share), length), :],
            share_recv.at[away, lax.rem(i, share)],
        )
        return owner, remote, local

    def send_share(source, target, i, away):
        owner, remote, local = share_copy(source, target, i, away)

        @pl.when(owner == section)
        def _():
            local.start()

        @pl.when(owner != section)
        def _():
            remote.start()

    def before_forward(i):
        @pl.when(section == 0)
        def _():
            load_rows(tokens, rows_in, i).wait()

        @pl.when(section > 0)
        def _():
            forward_copy(i).wait_recv()

    def after_forward(i):
        @pl.when(section < final)
        def _():
            forward_copy(i).start()

        @pl.when(section == final)
        def _():
            send_share(out, layer_out, i, 0)

    def before_backward(i):
        @pl.when(section == final)
        def _():
            load_rows(cotangent, grad, i).wait()

        @pl.when(section < final)
        def _():
            backward_copy(i).wait_recv()

    def after_backward(i):
        @pl.when(section > 0)
        def _():
            backward_copy(i).start()

        @pl.when(section == 0)
        def _():
            send_share(d_in, input_out, i, 1)

    lag = jnp.where(section == final, 0, jnp.where(section == final - 1, min(2, batches), batches))

    def ticks(forward, backward):
        def tick(t, carry):
            @pl.when(t < batches)
            def _():
                before_forward(t)
                forward(t)
                after_forward(t)

            late = t - lag

            @pl.when((late >= 0) & (late < batches))
            def _():
                before_backward(late)
                backward(late)
                after_backward(late)

            return carry

        lax.fori_loop(0, 2 * batches, tick, 0)

    def store(m, source, k):
        columns = aligned(k, width)
        return pltpu.make_async_copy(
            source.at[:, columns], weight_sums.at[m, :, columns], store_sem.at[m, k]
        )

    units = hidden // width

    @pl.when(is_attention)
    def _():
        load_weight.wait()
        for which in range(3):
            columns = slice(which * width, (which + 1) * width)
            down[:, columns] = weight[:, columns].T
        ticks(
            lambda i: attend_forward(i, gain, shift, refs),
            lambda i: attend_backward(i, gain, refs),
        )

        def unit(k, carry):
            columns = aligned(k, width)
            weight[:, columns] = dot_tn(rows_in[...], keep[:, columns]).astype(bf16)
            store(0, weight, k).start()
            return carry

        lax.fori_loop(0, units - 1, unit, 0)
        columns = slice(3 * width, 4 * width)
        weight[:, columns] = dot_tn(keep[:, columns], grad[...]).astype(bf16)
        store(0, weight, units - 1).start()

    @pl.when(is_feed)
    def _():
        load_weight.wait()
        load_down.wait()
        ticks(
            lambda i: feed_forward(aligned(i, length), gain, shift, refs),
            lambda i: feed_backward(aligned(i, length), gain, refs),
        )

        def unit(k, carry):
            columns = aligned(k, width)
            weight[:, columns] = dot_tn(rows_in[...], wide[:, columns]).astype(bf16)
            store(0, weight, k).start()
            down[:, columns] = dot_tn(grad[...], keep[:, columns]).astype(bf16)
            store(1, down, k).start()
            return carry

        lax.fori_loop(0, units, unit, 0)

    norm_out[...] = norm_sums[...]

    def drain(i, carry):
        @pl.when(section < final)
        def _():
            forward_copy(i).wait_send()

        @pl.when(section > 0)
        def _():
            backward_copy(i).wait_send()

        for away, source, target, sender in ((0, out, layer_out, final), (1, d_in, input_out, 0)):
            owner, remote, local = share_copy(source, target, i, away)

            @pl.when((section == sender) & (owner != section))
            def _():
                remote.wait_send()

            @pl.when(owner == section)
            def _():
                @pl.when(section == sender)
                def _():
                    local.wait()

                @pl.when(section != sender)
                def _():
                    remote.wait_recv()

        return carry

    lax.fori_loop(0, batches, drain, 0)
    for k in range(units):
        store(0, weight, k).wait()

    @pl.when(is_feed)
    def _():
        for k in range(units):
            store(1, down, k).wait()


def on_device(tokens, cotangent, segment_ids, first_weight, down_weight, ln_gain, ln_shift):
    sections = lax.axis_size("section")
    count, width = tokens.shape
    batches, length = segment_ids.shape
    hidden = first_weight.shape[2]
    units = hidden // width
    share = batches // sections
    any_space = pl.BlockSpec(memory_space=pl.ANY)
    vmem = pl.BlockSpec(memory_space=pltpu.VMEM)
    dma = pltpu.SemaphoreType.DMA
    layer_rows, input_rows, weight_sums, norm_sums = pl.pallas_call(
        functools.partial(pipeline, sections),
        out_shape=(
            jax.ShapeDtypeStruct((count // sections, width), bf16),
            jax.ShapeDtypeStruct((count // sections, width), bf16),
            jax.ShapeDtypeStruct((2, width, hidden), bf16),
            jax.ShapeDtypeStruct((2, 8, width), f32),
        ),
        in_specs=[any_space, any_space, vmem, any_space, any_space, vmem, vmem],
        out_specs=(any_space, any_space, any_space, vmem),
        scratch_shapes=[
            pltpu.VMEM((count, width), bf16),
            pltpu.VMEM((count, hidden), bf16),
            pltpu.VMEM((count, hidden), bf16),
            pltpu.VMEM((count, width), bf16),
            pltpu.VMEM((count, width), bf16),
            pltpu.VMEM((count, 1), f32),
            pltpu.VMEM((count, width), bf16),
            pltpu.VMEM((count, width), bf16),
            pltpu.VMEM((width, hidden), bf16),
            pltpu.VMEM((width, hidden), bf16),
            pltpu.VMEM((2, 8, width), f32),
            pltpu.VMEM((width, length), f32),
            pltpu.VMEM((batches * 16, length), f32),
            dma((2,)),
            dma((batches,)),
            dma((batches,)),
            dma((batches,)),
            dma((batches,)),
            dma((batches,)),
            dma((2, batches)),
            dma((2, share)),
            dma((2, units)),
        ],
        compiler_params=pltpu.CompilerParams(
            collective_id=0, has_side_effects=True, vmem_limit_bytes=64 * 2**20
        ),
    )(tokens, cotangent, segment_ids, first_weight, down_weight, ln_gain, ln_shift)
    has_down = lax.rem(lax.axis_index("section"), 2) == 1
    first_sum = lax.psum_scatter(weight_sums[0], "dp", scatter_dimension=1, tiled=True)
    down_sum = lax.psum_scatter(
        jnp.where(has_down, weight_sums[1], jnp.zeros_like(weight_sums[1])),
        "dp",
        scatter_dimension=1,
        tiled=True,
    )
    norm_sum = lax.psum_scatter(jnp.sum(norm_sums, axis=1), "dp", scatter_dimension=1, tiled=True)
    return (
        layer_rows,
        input_rows,
        first_sum.astype(f32)[None],
        down_sum.astype(f32)[None],
        norm_sum[0:1],
        norm_sum[1:2],
    )


def solution(mesh):
    return jax.shard_map(
        on_device,
        mesh=mesh,
        in_specs=(
            P("dp", None),
            P("dp", None),
            P("dp", None),
            P("section", None, None),
            P("section", None, None),
            P("section", None),
            P("section", None),
        ),
        out_specs=(
            P(("dp", "section"), None),
            P(("dp", "section"), None),
            P("section", None, "dp"),
            P("section", None, "dp"),
            P("section", "dp"),
            P("section", "dp"),
        ),
        check_vma=False,
    )
```

```python
import functools

import jax
import jax.numpy as jnp
from jax import lax
from jax.experimental import pallas as pl
from jax.experimental.pallas import tpu as pltpu
from jax.sharding import PartitionSpec as P

HEADS = 12
NORM_EPSILON = 1e-12
MASKED_SCORE = -1e30
INV_SQRT2 = 0.7071067811865476
INV_SQRT2PI = 0.3989422804014327
MESH = pl.DeviceIdType.MESH
bf16 = jnp.bfloat16
f32 = jnp.float32


def dot(a, b):
    return jnp.dot(a, b, preferred_element_type=f32)


def dot_nt(a, b):
    return lax.dot_general(a, b, (((1,), (1,)), ((), ())), preferred_element_type=f32)


def dot_tn(a, b):
    return lax.dot_general(a, b, (((0,), (0,)), ((), ())), preferred_element_type=f32)


def aligned(index, size):
    return pl.ds(pl.multiple_of(index * size, size), size)


def norm_forward(residual, rows, gain, shift, refs):
    mean = jnp.mean(residual, axis=-1, keepdims=True)
    centered = residual - mean
    spread = jnp.mean(centered * centered, axis=-1, keepdims=True)
    scale = lax.rsqrt(spread + NORM_EPSILON)
    normal = centered * scale
    refs.normal[rows, :] = normal.astype(bf16)
    refs.scale[rows, :] = scale
    refs.out[rows, :] = (normal * gain + shift).astype(bf16)


def norm_backward(rows, gain, refs):
    upstream = refs.grad[rows, :].astype(f32)
    normal = refs.normal[rows, :].astype(f32)
    scale = refs.scale[rows, :]
    count, width = upstream.shape
    refs.norm_sums[0] += jnp.sum((upstream * normal).reshape(count // 8, 8, width), axis=0)
    refs.norm_sums[1] += jnp.sum(upstream.reshape(count // 8, 8, width), axis=0)
    pulled = upstream * gain
    mean = jnp.mean(pulled, axis=-1, keepdims=True)
    along = jnp.mean(pulled * normal, axis=-1, keepdims=True)
    d_resid = scale * (pulled - mean - normal * along)
    refs.grad[rows, :] = d_resid.astype(bf16)
    return d_resid


def feed_forward(rows, gain, shift, refs):
    width, hidden = refs.weight.shape
    tile = width
    tiles = hidden // tile
    source = refs.rows_in[rows, :]
    residual = source.astype(f32)

    def up(t):
        return dot(source, refs.weight[:, t * tile : (t + 1) * tile])

    def down(value, t):
        return dot_nt(value, refs.down[:, t * tile : (t + 1) * tile])

    pre = up(0)
    held = None
    for t in range(tiles):
        following = up(t + 1) if t + 1 < tiles else None
        cdf = 0.5 + 0.5 * lax.erf(pre * INV_SQRT2)
        value = (pre * cdf).astype(bf16)
        slope = cdf + pre * (INV_SQRT2PI * jnp.exp(-0.5 * pre * pre))
        refs.keep[rows, t * tile : (t + 1) * tile] = value
        refs.wide[rows, t * tile : (t + 1) * tile] = slope.astype(bf16)
        if held is not None:
            residual = residual + down(held, t - 1)
        held, pre = value, following
    residual = residual + down(held, tiles - 1)
    norm_forward(residual, rows, gain, shift, refs)


def feed_backward(rows, gain, refs):
    width, hidden = refs.weight.shape
    tile = width
    tiles = hidden // tile
    d_resid = norm_backward(rows, gain, refs)
    d_branch = d_resid.astype(bf16)
    total = d_resid

    def up(t):
        return dot(d_branch, refs.down[:, t * tile : (t + 1) * tile])

    def down(value, t):
        return dot_nt(value, refs.weight[:, t * tile : (t + 1) * tile])

    d_hidden = up(0)
    held = None
    for t in range(tiles):
        following = up(t + 1) if t + 1 < tiles else None
        columns = slice(t * tile, (t + 1) * tile)
        d_pre = (d_hidden * refs.wide[rows, columns].astype(f32)).astype(bf16)
        refs.wide[rows, columns] = d_pre
        if held is not None:
            total = total + down(held, t - 1)
        held, d_hidden = d_pre, following
    total = total + down(held, tiles - 1)
    refs.d_in[rows, :] = total.astype(bf16)


def head_part(refs, first_row, length, blocks, which, n):
    head_width = refs.weight.shape[0] // HEADS
    per_block = length // head_width
    column = (which * blocks + n // per_block) * length
    rows = pl.ds(pl.multiple_of(first_row + (n % per_block) * head_width, head_width), head_width)
    return rows, slice(column, column + length)


def attend_forward(index, gain, shift, refs):
    length = refs.segments.shape[1]
    width = refs.weight.shape[0]
    blocks = width // length
    rows = aligned(index, length)
    first_row = index * length
    source = refs.rows_in[rows, :]
    ids = jnp.broadcast_to(refs.segments[pl.ds(index, 1), :].astype(f32), (length, length))
    allowed = ids == ids.T
    score_scale = (width // HEADS) ** (-0.5)
    for which in range(3):
        turned = dot_nt(refs.down[:, which * width : (which + 1) * width], source)
        if which == 0:
            turned = turned * score_scale
        turned = turned.astype(bf16)
        for j in range(blocks):
            column = (which * blocks + j) * length
            refs.keep[rows, column : column + length] = turned[j * length : (j + 1) * length, :]
    place = functools.partial(head_part, refs, first_row, length, blocks)

    def score(n):
        return dot_tn(refs.keep[place(1, n)], refs.keep[place(0, n)])

    def weigh(scores):
        scores = jnp.where(allowed, scores, MASKED_SCORE)
        raw = jnp.exp(scores - jnp.max(scores, axis=0, keepdims=True))
        return raw.astype(bf16), 1.0 / jnp.sum(raw, axis=0, keepdims=True)

    def finish(n, raw, inverse):
        refs.wide[rows, n * length : (n + 1) * length] = raw
        refs.inverse[pl.ds(index * 16 + n, 1), :] = inverse
        refs.keep[place(3, n)] = (dot(refs.keep[place(2, n)], raw) * inverse).astype(bf16)

    ahead = 2
    scores = [score(n) for n in range(ahead)]
    held = None
    for n in range(HEADS):
        if n + ahead < HEADS:
            scores.append(score(n + ahead))
        current = weigh(scores[n])
        if held is not None:
            finish(n - 1, *held)
        held = current
    finish(HEADS - 1, *held)
    residual = source.astype(f32)
    for j in range(blocks):
        column = (3 * blocks + j) * length
        residual = residual + dot_tn(
            refs.keep[rows, column : column + length],
            refs.weight[j * length : (j + 1) * length, 3 * width :],
        )
    norm_forward(residual, rows, gain, shift, refs)


def attend_backward(index, gain, refs):
    length = refs.segments.shape[1]
    width = refs.weight.shape[0]
    head_width = width // HEADS
    blocks = width // length
    per_block = length // head_width
    score_scale = head_width ** (-0.5)
    rows = aligned(index, length)
    first_row = index * length
    d_resid = norm_backward(rows, gain, refs)
    refs.d_context[:, :length] = dot_nt(refs.weight[:, 3 * width :], d_resid.astype(bf16))
    place = functools.partial(head_part, refs, first_row, length, blocks)

    def first(n):
        inverse = refs.inverse[pl.ds(index * 16 + n, 1), :]
        d_context = refs.d_context[n * head_width : (n + 1) * head_width, :length] * inverse
        along = jnp.sum(d_context * refs.keep[place(3, n)].astype(f32), axis=0, keepdims=True)
        d_context = d_context.astype(bf16)
        return dot_tn(refs.keep[place(2, n)], d_context), along, d_context

    def second(n, d_probs, along, d_context):
        raw = refs.wide[rows, n * length : (n + 1) * length]
        return (raw.astype(f32) * (d_probs - along)).astype(bf16), raw, d_context

    made = ([], [], [])

    def third(n, d_scores, raw, d_context):
        made[0].append(dot(refs.keep[place(1, n)], d_scores) * score_scale)
        made[1].append(dot_nt(refs.keep[place(0, n)], d_scores))
        made[2].append(dot_nt(d_context, raw))
        if n % per_block == per_block - 1:
            block = n // per_block
            for which in range(3):
                column = (which * blocks + block) * length
                whole = jnp.concatenate(made[which], axis=0).astype(bf16)
                refs.keep[rows, column : column + length] = whole.T
                made[which].clear()
            column = (3 * blocks + block) * length
            refs.keep[rows, column : column + length] = refs.keep[rows, column : column + length].T

    current = first(0)
    held = None
    for n in range(HEADS):
        following = first(n + 1) if n + 1 < HEADS else None
        ready = second(n, *current)
        if held is not None:
            third(n - 1, *held)
        held, current = ready, following
    third(HEADS - 1, *held)
    d_in = d_resid + dot_nt(refs.keep[rows, : 3 * width], refs.weight[:, : 3 * width])
    refs.d_in[rows, :] = d_in.astype(bf16)


class Refs:
    def __init__(self, **named):
        self.__dict__.update(named)


def pipeline(
    sections,
    levels,
    tokens,
    cotangent,
    segments,
    weight_in,
    down_in,
    gain_in,
    shift_in,
    layer_out,
    input_out,
    first_out,
    down_out,
    norm_out,
    rows_in,
    keep,
    wide,
    grad,
    normal,
    scale,
    out,
    d_in,
    weight,
    down,
    norm_sums,
    d_context,
    inverse,
    load_sem,
    first_sem,
    forward_send,
    forward_recv,
    backward_send,
    backward_recv,
    share_send,
    share_recv,
    store_sem,
    level_recv=None,
    norm_recv=None,
    norm_send=None,
    ready_sem=None,
    pair_sems=None,
    level_sems=None,
    norm_sems=None,
):
    dp = lax.axis_index("dp")
    section = lax.axis_index("section")
    batches, length = segments.shape
    width, hidden = weight.shape
    share = batches // sections
    final = sections - 1
    refs = Refs(
        rows_in=rows_in, keep=keep, wide=wide, grad=grad, normal=normal, scale=scale, out=out, d_in=d_in,
        weight=weight, down=down, norm_sums=norm_sums, d_context=d_context, inverse=inverse, segments=segments,
    )
    is_attention = lax.rem(section, 2) == 0
    is_feed = lax.rem(section, 2) == 1

    def load_rows(source, target, i):
        rows = aligned(i, length)
        return pltpu.make_async_copy(source.at[rows, :], target.at[rows, :], first_sem.at[i])

    load_weight = pltpu.make_async_copy(weight_in.at[0], weight, load_sem.at[0])
    load_down = pltpu.make_async_copy(down_in.at[0], down, load_sem.at[1])
    load_weight.start()

    @pl.when(is_feed)
    def _():
        load_down.start()

    @pl.when(section == 0)
    def _():
        for i in range(batches):
            load_rows(tokens, rows_in, i).start()

    @pl.when(section == final)
    def _():
        for i in range(batches):
            load_rows(cotangent, grad, i).start()

    barrier = pltpu.get_barrier_semaphore()
    for other in range(1, sections):
        pl.semaphore_signal(
            barrier, inc=1, device_id=(dp, lax.rem(section + other, sections)), device_id_type=MESH
        )
    if levels:
        pair, level = lax.rem(dp, 2), dp // 2
        partner = dp + 1 - 2 * pair
        pl.semaphore_signal(barrier, inc=1, device_id=(partner, section), device_id_type=MESH)
        peers = [lax.rem(dp + 2 * other, 2 * levels) for other in range(1, levels)]
        for peer in peers:
            pl.semaphore_signal(barrier, inc=1, device_id=(peer, section), device_id_type=MESH)
        pl.semaphore_wait(barrier, sections - 1 + levels)
    else:
        pl.semaphore_wait(barrier, sections - 1)

    norm_sums[...] = jnp.zeros_like(norm_sums)
    gain = gain_in[...]
    shift = shift_in[...]

    def forward_copy(i):
        rows = aligned(i, length)
        return pltpu.make_async_remote_copy(
            out.at[rows, :], rows_in.at[rows, :], forward_send.at[i], forward_recv.at[i],
            device_id=(dp, lax.rem(section + 1, sections)), device_id_type=MESH,
        )

    def backward_copy(i):
        rows = aligned(i, length)
        return pltpu.make_async_remote_copy(
            d_in.at[rows, :], grad.at[rows, :], backward_send.at[i], backward_recv.at[i],
            device_id=(dp, lax.rem(section + sections - 1, sections)), device_id_type=MESH,
        )

    def share_copy(source, target, i, away):
        owner = i // share
        remote = pltpu.make_async_remote_copy(
            source.at[aligned(i, length), :], target.at[aligned(lax.rem(i, share), length), :],
            share_send.at[away, i], share_recv.at[away, lax.rem(i, share)],
            device_id=(dp, owner), device_id_type=MESH,
        )
        local = pltpu.make_async_copy(
            source.at[aligned(i, length), :], target.at[aligned(lax.rem(i, share), length), :],
            share_recv.at[away, lax.rem(i, share)],
        )
        return owner, remote, local

    def send_share(source, target, i, away):
        owner, remote, local = share_copy(source, target, i, away)

        @pl.when(owner == section)
        def _():
            local.start()

        @pl.when(owner != section)
        def _():
            remote.start()

    def before_forward(i):
        @pl.when(section == 0)
        def _():
            load_rows(tokens, rows_in, i).wait()

        @pl.when(section > 0)
        def _():
            forward_copy(i).wait_recv()

    def after_forward(i):
        @pl.when(section < final)
        def _():
            forward_copy(i).start()

    def before_backward(i):
        @pl.when(section == final)
        def _():
            load_rows(cotangent, grad, i).wait()

        @pl.when(section < final)
        def _():
            backward_copy(i).wait_recv()

    def after_backward(i):
        @pl.when(section > 0)
        def _():
            backward_copy(i).start()

        @pl.when(section == 0)
        def _():
            send_share(d_in, input_out, i, 1)

    lag = jnp.where(section == final, 0, jnp.where(section == final - 1, min(2, batches), batches))

    mask = (1 << (batches - 1).bit_length()) - 1

    def ticks(forward, backward):
        def tick(t, carry):
            @pl.when(t < batches)
            def _():
                i = t & mask
                before_forward(i)
                forward(i)
                after_forward(i)

            late = t - lag

            @pl.when((late >= 0) & (late < batches))
            def _():
                i = late & mask
                before_backward(i)
                backward(i)
                after_backward(i)

            return carry

        lax.fori_loop(0, 2 * batches, tick, 0)

    units = hidden // width

    def gradient_rows_left():
        @pl.when(section > 0)
        def _():
            def one(i, carry):
                backward_copy(i).wait_send()
                return carry

            lax.fori_loop(0, batches, one, 0)

    def send_output():
        @pl.when(section == final)
        def _():
            def one(i, carry):
                send_share(out, layer_out, i, 0)
                return carry

            lax.fori_loop(0, batches, one, 0)

    def drain():
        def one(i, carry):
            @pl.when(section < final)
            def _():
                forward_copy(i).wait_send()

            @pl.when((section > 0) & is_attention)
            def _():
                backward_copy(i).wait_send()

            for away, source, target, sender in ((0, out, layer_out, final), (1, d_in, input_out, 0)):
                owner, remote, local = share_copy(source, target, i, away)

                @pl.when((section == sender) & (owner != section))
                def _():
                    remote.wait_send()

                @pl.when((section == sender) & (owner == section))
                def _():
                    local.wait()

                @pl.when((section != sender) & (owner == section))
                def _():
                    remote.wait_recv()

            return carry

        lax.fori_loop(0, batches, one, 0)

    def plain_gradients(parts, late, line_first=()):
        def store(m, source, target, k):
            columns = aligned(k, width)
            return pltpu.make_async_copy(
                source.at[:, columns], target.at[:, columns], store_sem.at[m, k]
            )

        for m, (make, source, _, target) in enumerate(parts):

            def unit(k, carry):
                make(k)
                store(m, source, target, k).start()
                return carry

            lax.fori_loop(0, units, unit, 0)
        send_output()
        norm_out[...] = jnp.sum(norm_sums[...], axis=1)
        for m, (make, source, _, target) in enumerate(parts):
            for k in range(units):
                store(m, source, target, k).wait()

    def summed_gradients(parts, late, line_first=()):
        columns_out = hidden // (2 * levels)
        halves = 2
        part_rows = width // halves

        above, below = levels - 1 - level, level

        def level_of(j):
            near_low = jnp.where(j < above, levels - 1 - j, j - above)
            near_high = jnp.where(j < below, j, levels - 1 - (j - below))
            moving = jnp.where(level < levels // 2, near_low, near_high)
            return jnp.where(j == levels - 1, level, moving)

        def half_of(source, k, side, h):
            column = pl.multiple_of(k * width + side * columns_out, columns_out)
            return source.at[pl.ds(h * part_rows, part_rows), pl.ds(column, columns_out)]

        def pair_slot(landing, k, h):
            row = pl.multiple_of((k // 2) * width + h * part_rows, part_rows)
            column = pl.multiple_of(lax.rem(k, 2) * columns_out, columns_out)
            return landing.at[pl.ds(row, part_rows), pl.ds(column, columns_out)]

        def pair_copy(m, k, h):
            _, source, landing, _ = parts[m]
            return pltpu.make_async_remote_copy(
                half_of(source, k, 1 - pair, h), pair_slot(landing, k, h),
                pair_sems.at[0, m, k, h], pair_sems.at[1, m, k, h],
                device_id=(partner, section), device_id_type=MESH,
            )

        def level_slot(m, slot, h):
            return level_recv.at[m, slot, pl.ds(h * part_rows, part_rows), :]

        def level_copy(m, k, h, other=False):
            step = jnp.where(k > level, 1, -1)
            slot = jnp.where(k == level - 1, levels, k)
            side = 1 - pair if other else pair
            place = 1 if other else m
            return pltpu.make_async_remote_copy(
                half_of(parts[m][1], k, side, h), level_slot(place, slot, h),
                level_sems.at[0, place, k, h], level_sems.at[1, place, slot, h],
                device_id=(dp + 2 * step, section), device_id_type=MESH,
            )

        def arrival(m, slot, h):
            return pltpu.make_async_copy(
                level_slot(m, slot, h), level_slot(m, slot, h), level_sems.at[1, m, slot, h]
            )

        def make_unit(m, k):
            parts[m][0](k)
            for h in range(halves):
                if h not in line_first:
                    pair_copy(m, k, h).start()

        def pass_on(m, k, h, mine, total, other=False):
            from_below = (k > level) & (level > 0)
            from_above = (k < level) & (level < levels - 1)
            moving = from_below | from_above
            place = 1 if other else m

            @pl.when(moving)
            def _():
                arrival(place, k, h).wait()
                mine[...] = (total() + level_slot(place, k, h)[...].astype(f32)).astype(bf16)

            @pl.when(jnp.logical_not(moving))
            def _():
                mine[...] = total().astype(bf16)

            @pl.when(k != level)
            def _():
                level_copy(m, k, h, other).start()

        def pass_unit(m, k):
            _, source, landing, _ = parts[m]
            for h in line_first:

                @pl.when(k != level)
                def _():
                    for other in (False, True):
                        mine = half_of(source, k, 1 - pair if other else pair, h)
                        pass_on(m, k, h, mine, lambda: mine[...].astype(f32), other)

            for h in range(halves):
                if h in line_first:
                    continue
                pair_copy(m, k, h).wait_recv()
                mine = half_of(source, k, pair, h)
                theirs = pair_slot(landing, k, h)
                pass_on(m, k, h, mine, lambda: mine[...].astype(f32) + theirs[...].astype(f32))

        def gather(m, h, other=False):
            place = 1 if other else m
            side = 1 - pair if other else pair
            wanted = d_context.at[pl.ds(h * part_rows, part_rows), pl.ds(0, columns_out)]
            wanted[...] = half_of(parts[m][1], level, side, h)[...].astype(f32)
            for there, slot in ((level > 0, level), (level < levels - 1, levels)):

                @pl.when(there)
                def _():
                    arrival(place, slot, h).wait()
                    wanted[...] += level_slot(place, slot, h)[...].astype(f32)

            return wanted

        def last_unit(m):
            _, source, landing, target = parts[m]
            for h in line_first:
                half_of(source, level, 1 - pair, h)[...] = gather(m, h, True)[...].astype(bf16)
                pair_copy(m, level, h).start()
            copies = []
            for h in [h for h in range(halves) if h not in line_first] + list(line_first):
                wanted = gather(m, h)
                if h in line_first:
                    pair_copy(m, level, h).wait_recv()
                    wanted[...] += pair_slot(landing, level, h)[...].astype(f32)
                rows = pl.ds(h * part_rows, part_rows)
                copies.append(pltpu.make_async_copy(wanted, target.at[0, rows, :], store_sem.at[m, h]))
                copies[-1].start()
            for copy in copies:
                copy.wait()

        def norm_copy(way, device):
            return pltpu.make_async_remote_copy(
                norm_send.at[min(way, 1)], norm_recv.at[way], norm_sems.at[0, way], norm_sems.at[1, way],
                device_id=(device, section), device_id_type=MESH,
            )

        def start_norms():
            norm_send[0] = jnp.concatenate(
                [jnp.sum(norm_sums[...], axis=1), jnp.zeros((6, width), f32)], axis=0
            )
            norm_copy(0, partner).start()

        def spread_norms():
            norm_copy(0, partner).wait_recv()
            norm_send[1] = norm_send[0] + norm_recv[0]
            for way, peer in enumerate(peers, 1):
                norm_copy(way, peer).start()

        def finish_norms():
            total = norm_send[1]
            for way, peer in enumerate(peers, 1):
                norm_copy(way, peer).wait_recv()
                total = total + norm_recv[way]
            norm_out[...] = total
            norm_copy(0, partner).wait_send()
            for way, peer in enumerate(peers, 1):
                norm_copy(way, peer).wait_send()

        start_norms()
        pl.semaphore_signal(ready_sem, inc=1, device_id=(partner, section), device_id_type=MESH)
        pl.semaphore_wait(ready_sem, 1)
        total_units = len(parts) * units

        def of_unit(t, act):
            for m in range(len(parts)):

                @pl.when(t // units == m)
                def _():
                    act(m, level_of(lax.rem(t, units)))

        def turn(t, carry):
            @pl.when(t < total_units)
            def _():
                of_unit(t, make_unit)

            @pl.when(t == 0)
            def _():
                spread_norms()

            @pl.when(t >= late)
            def _():
                of_unit(t - late, pass_unit)

            return carry

        lax.fori_loop(0, total_units, turn, 0)
        send_output()
        lax.fori_loop(total_units, total_units + late, turn, 0)
        for m in range(len(parts)):
            last_unit(m)
        finish_norms()

        def sent(k, carry):
            for m in range(len(parts)):
                for h in range(halves):
                    if h not in line_first:
                        pair_copy(m, k, h).wait_send()

                    @pl.when(k != level)
                    def _():
                        level_copy(m, k, h).wait_send()
                        if h in line_first:
                            level_copy(m, k, h, True).wait_send()

            return carry

        lax.fori_loop(0, units, sent, 0)
        for m in range(len(parts)):
            for h in line_first:
                pair_copy(m, level, h).wait_send()

    weight_gradients = summed_gradients if levels else plain_gradients

    @pl.when(is_attention)
    def _():
        if levels:
            d_context[...] = jnp.zeros_like(d_context)
            zeros = pltpu.make_async_copy(
                d_context.at[:, pl.ds(0, hidden // (2 * levels))], down_out.at[0], load_sem.at[1]
            )
            zeros.start()
            zeros.wait()
        load_weight.wait()
        for which in range(3):
            columns = slice(which * width, (which + 1) * width)
            down[:, columns] = weight[:, columns].T
        ticks(
            lambda i: attend_forward(i, gain, shift, refs),
            lambda i: attend_backward(i, gain, refs),
        )

        def first(k):
            columns = aligned(k, width)

            @pl.when(k < units - 1)
            def _():
                weight[:, columns] = dot_tn(rows_in[...], keep[:, columns]).astype(bf16)

            @pl.when(k == units - 1)
            def _():
                weight[:, columns] = dot_tn(keep[:, columns], grad[...]).astype(bf16)

        weight_gradients(((first, weight, normal, first_out),), 1, (0,))

    @pl.when(is_feed)
    def _():
        load_weight.wait()
        load_down.wait()
        ticks(
            lambda i: feed_forward(aligned(i, length), gain, shift, refs),
            lambda i: feed_backward(aligned(i, length), gain, refs),
        )

        gradient_rows_left()

        def first(k):
            columns = aligned(k, width)
            weight[:, columns] = dot_tn(rows_in[...], wide[:, columns]).astype(bf16)

        def second(k):
            columns = aligned(k, width)
            down[:, columns] = dot_tn(grad[...], keep[:, columns]).astype(bf16)

        weight_gradients(
            ((first, weight, normal, first_out), (second, down, d_in, down_out)), 2
        )

    drain()


def on_device(tokens, cotangent, segment_ids, first_weight, down_weight, ln_gain, ln_shift):
    sections = lax.axis_size("section")
    groups = lax.axis_size("dp")
    count, width = tokens.shape
    batches, length = segment_ids.shape
    hidden = first_weight.shape[2]
    units = hidden // width
    share = batches // sections
    levels = units if groups == 2 * units and (units + 1) // 2 * width <= count else 0
    columns_out = hidden // groups
    any_space = pl.BlockSpec(memory_space=pl.ANY)
    vmem = pl.BlockSpec(memory_space=pltpu.VMEM)
    dma = pltpu.SemaphoreType.DMA
    if levels:
        sums = [jax.ShapeDtypeStruct((1, width, columns_out), f32)] * 2
        sums.append(jax.ShapeDtypeStruct((8, width), f32))
    else:
        sums = [jax.ShapeDtypeStruct((width, hidden), bf16)] * 2
        sums.append(jax.ShapeDtypeStruct((2, width), f32))
    scratch = [
        pltpu.VMEM((count, width), bf16),
        pltpu.VMEM((count, hidden), bf16),
        pltpu.VMEM((count, hidden), bf16),
        pltpu.VMEM((count, width), bf16),
        pltpu.VMEM((count, width), bf16),
        pltpu.VMEM((count, 1), f32),
        pltpu.VMEM((count, width), bf16),
        pltpu.VMEM((count, width), bf16),
        pltpu.VMEM((width, hidden), bf16),
        pltpu.VMEM((width, hidden), bf16),
        pltpu.VMEM((2, 8, width), f32),
        pltpu.VMEM((width, max(length, columns_out if levels else 0)), f32),
        pltpu.VMEM((batches * 16, length), f32),
        dma((2,)),
        dma((batches,)),
        dma((batches,)),
        dma((batches,)),
        dma((batches,)),
        dma((batches,)),
        dma((2, batches)),
        dma((2, share)),
        dma((2, units)),
    ]
    if levels:
        scratch += [
            pltpu.VMEM((2, levels + 1, width, columns_out), bf16),
            pltpu.VMEM((levels, 8, width), f32),
            pltpu.VMEM((2, 8, width), f32),
            pltpu.SemaphoreType.REGULAR,
            dma((2, 2, levels, 2)),
            dma((2, 2, levels + 1, 2)),
            dma((2, levels)),
        ]
    layer_rows, input_rows, first_sum, down_sum, norm_sum = pl.pallas_call(
        functools.partial(pipeline, sections, levels),
        out_shape=(
            jax.ShapeDtypeStruct((count // sections, width), bf16),
            jax.ShapeDtypeStruct((count // sections, width), bf16),
            *sums,
        ),
        in_specs=[any_space, any_space, vmem, any_space, any_space, vmem, vmem],
        out_specs=(any_space, any_space, any_space, any_space, vmem),
        scratch_shapes=scratch,
        compiler_params=pltpu.CompilerParams(
            collective_id=0, has_side_effects=True, vmem_limit_bytes=64 * 2**20
        ),
    )(tokens, cotangent, segment_ids, first_weight, down_weight, ln_gain, ln_shift)
    if levels:
        own = width // groups
        norm_sum = lax.dynamic_slice_in_dim(norm_sum, lax.axis_index("dp") * own, own, 1)
    else:
        has_down = lax.rem(lax.axis_index("section"), 2) == 1
        down_sum = jnp.where(has_down, down_sum, jnp.zeros_like(down_sum))
        first_sum, down_sum, norm_sum = (
            lax.psum_scatter(value, "dp", scatter_dimension=1, tiled=True)
            for value in (first_sum, down_sum, norm_sum)
        )
        first_sum, down_sum = first_sum.astype(f32)[None], down_sum.astype(f32)[None]
    return (layer_rows, input_rows, first_sum, down_sum, norm_sum[0:1], norm_sum[1:2])


def solution(mesh):
    return jax.shard_map(
        on_device,
        mesh=mesh,
        in_specs=(
            P("dp", None),
            P("dp", None),
            P("dp", None),
            P("section", None, None),
            P("section", None, None),
            P("section", None),
            P("section", None),
        ),
        out_specs=(
            P(("dp", "section"), None),
            P(("dp", "section"), None),
            P("section", None, "dp"),
            P("section", None, "dp"),
            P("section", "dp"),
            P("section", "dp"),
        ),
        check_vma=False,
    )
```

```python
import functools

import jax
import jax.numpy as jnp
from jax import lax
from jax.experimental import pallas as pl
from jax.experimental.pallas import tpu as pltpu
from jax.sharding import PartitionSpec as P

HEADS = 12
HALVES = 4
NORM_EPSILON = 1e-12
MASKED_SCORE = -1e30
INV_SQRT2 = 0.7071067811865476
INV_SQRT2PI = 0.3989422804014327
MESH = pl.DeviceIdType.MESH
bf16 = jnp.bfloat16
f32 = jnp.float32


def dot(a, b):
    return jnp.dot(a, b, preferred_element_type=f32)


def dot_nt(a, b):
    return lax.dot_general(a, b, (((1,), (1,)), ((), ())), preferred_element_type=f32)


def dot_tn(a, b):
    return lax.dot_general(a, b, (((0,), (0,)), ((), ())), preferred_element_type=f32)


def aligned(index, size):
    return pl.ds(pl.multiple_of(index * size, size), size)


def norm_forward(residual, rows, gain, shift, refs):
    mean = jnp.mean(residual, axis=-1, keepdims=True)
    centered = residual - mean
    spread = jnp.mean(centered * centered, axis=-1, keepdims=True)
    scale = lax.rsqrt(spread + NORM_EPSILON)
    normal = centered * scale
    refs.normal[rows, :] = normal.astype(bf16)
    refs.scale[rows, :] = scale
    refs.out[rows, :] = (normal * gain + shift).astype(bf16)


def norm_backward(rows, gain, refs):
    upstream = refs.grad[rows, :].astype(f32)
    normal = refs.normal[rows, :].astype(f32)
    scale = refs.scale[rows, :]
    count, width = upstream.shape
    refs.norm_sums[0] += jnp.sum((upstream * normal).reshape(count // 8, 8, width), axis=0)
    refs.norm_sums[1] += jnp.sum(upstream.reshape(count // 8, 8, width), axis=0)
    pulled = upstream * gain
    mean = jnp.mean(pulled, axis=-1, keepdims=True)
    along = jnp.mean(pulled * normal, axis=-1, keepdims=True)
    d_resid = scale * (pulled - mean - normal * along)
    refs.grad[rows, :] = d_resid.astype(bf16)
    return d_resid


def feed_forward(rows, gain, shift, refs):
    width, hidden = refs.weight.shape
    tile = width
    tiles = hidden // tile
    source = refs.rows_in[rows, :]
    residual = source.astype(f32)

    def up(t):
        return dot(source, refs.weight[:, t * tile : (t + 1) * tile])

    def down(value, t):
        return dot_nt(value, refs.down[:, t * tile : (t + 1) * tile])

    pre = up(0)
    held = None
    for t in range(tiles):
        following = up(t + 1) if t + 1 < tiles else None
        cdf = 0.5 + 0.5 * lax.erf(pre * INV_SQRT2)
        value = (pre * cdf).astype(bf16)
        slope = cdf + pre * (INV_SQRT2PI * jnp.exp(-0.5 * pre * pre))
        refs.keep[rows, t * tile : (t + 1) * tile] = value
        refs.wide[rows, t * tile : (t + 1) * tile] = slope.astype(bf16)
        if held is not None:
            residual = residual + down(held, t - 1)
        held, pre = value, following
    residual = residual + down(held, tiles - 1)
    norm_forward(residual, rows, gain, shift, refs)


def feed_backward(rows, gain, refs):
    width, hidden = refs.weight.shape
    tile = width
    tiles = hidden // tile
    d_resid = norm_backward(rows, gain, refs)
    d_branch = d_resid.astype(bf16)
    total = d_resid

    def up(t):
        return dot(d_branch, refs.down[:, t * tile : (t + 1) * tile])

    def down(value, t):
        return dot_nt(value, refs.weight[:, t * tile : (t + 1) * tile])

    d_hidden = up(0)
    held = None
    for t in range(tiles):
        following = up(t + 1) if t + 1 < tiles else None
        columns = slice(t * tile, (t + 1) * tile)
        d_pre = (d_hidden * refs.wide[rows, columns].astype(f32)).astype(bf16)
        refs.wide[rows, columns] = d_pre
        if held is not None:
            total = total + down(held, t - 1)
        held, d_hidden = d_pre, following
    total = total + down(held, tiles - 1)
    refs.d_in[rows, :] = total.astype(bf16)


def head_part(refs, first_row, length, blocks, which, n):
    head_width = refs.weight.shape[0] // HEADS
    per_block = length // head_width
    column = (which * blocks + n // per_block) * length
    rows = pl.ds(pl.multiple_of(first_row + (n % per_block) * head_width, head_width), head_width)
    return rows, slice(column, column + length)


def attend_forward(index, gain, shift, refs):
    length = refs.segments.shape[1]
    width = refs.weight.shape[0]
    blocks = width // length
    rows = aligned(index, length)
    first_row = index * length
    source = refs.rows_in[rows, :]
    ids = jnp.broadcast_to(refs.segments[pl.ds(index, 1), :].astype(f32), (length, length))
    allowed = ids == ids.T
    score_scale = (width // HEADS) ** (-0.5)
    for which in range(3):
        turned = dot_nt(refs.down[:, which * width : (which + 1) * width], source)
        if which == 0:
            turned = turned * score_scale
        turned = turned.astype(bf16)
        for j in range(blocks):
            column = (which * blocks + j) * length
            refs.keep[rows, column : column + length] = turned[j * length : (j + 1) * length, :]
    place = functools.partial(head_part, refs, first_row, length, blocks)

    def score(n):
        return dot_tn(refs.keep[place(1, n)], refs.keep[place(0, n)])

    def weigh(scores):
        scores = jnp.where(allowed, scores, MASKED_SCORE)
        raw = jnp.exp(scores - jnp.max(scores, axis=0, keepdims=True))
        return raw.astype(bf16), 1.0 / jnp.sum(raw, axis=0, keepdims=True)

    def finish(n, raw, inverse):
        refs.wide[rows, n * length : (n + 1) * length] = raw
        refs.inverse[pl.ds(index * 16 + n, 1), :] = inverse
        refs.keep[place(3, n)] = (dot(refs.keep[place(2, n)], raw) * inverse).astype(bf16)

    ahead = 3
    scores = [score(n) for n in range(ahead)]
    held = None
    for n in range(HEADS):
        if n + ahead < HEADS:
            scores.append(score(n + ahead))
        current = weigh(scores[n])
        if held is not None:
            finish(n - 1, *held)
        held = current
    finish(HEADS - 1, *held)
    residual = source.astype(f32)
    for j in range(blocks):
        column = (3 * blocks + j) * length
        residual = residual + dot_tn(
            refs.keep[rows, column : column + length],
            refs.weight[j * length : (j + 1) * length, 3 * width :],
        )
    norm_forward(residual, rows, gain, shift, refs)


def attend_backward(index, gain, refs):
    length = refs.segments.shape[1]
    width = refs.weight.shape[0]
    head_width = width // HEADS
    blocks = width // length
    per_block = length // head_width
    score_scale = head_width ** (-0.5)
    rows = aligned(index, length)
    first_row = index * length
    d_resid = norm_backward(rows, gain, refs)
    d_branch = d_resid.astype(bf16)
    total = d_resid

    def unmix(j):
        some = slice(j * length, (j + 1) * length)
        refs.d_context[some, :] = dot_nt(refs.weight[some, 3 * width :], d_branch)

    def unproject(j):
        some = [slice((which * blocks + j) * length, (which * blocks + j + 1) * length) for which in range(3)]
        left = jnp.concatenate([refs.keep[rows, part] for part in some], axis=1)
        right = jnp.concatenate([refs.weight[:, part] for part in some], axis=1)
        return dot_nt(left, right)

    unmix(0)
    place = functools.partial(head_part, refs, first_row, length, blocks)

    def first(n):
        inverse = refs.inverse[pl.ds(index * 16 + n, 1), :]
        d_context = refs.d_context[n * head_width : (n + 1) * head_width, :] * inverse
        along = jnp.sum(d_context * refs.keep[place(3, n)].astype(f32), axis=0, keepdims=True)
        d_context = d_context.astype(bf16)
        return dot_tn(refs.keep[place(2, n)], d_context), along, d_context

    def second(n, d_probs, along, d_context):
        raw = refs.wide[rows, n * length : (n + 1) * length]
        return (raw.astype(f32) * (d_probs - along)).astype(bf16), raw, d_context

    made = ([], [], [])

    def third(n, d_scores, raw, d_context):
        made[0].append(dot(refs.keep[place(1, n)], d_scores) * score_scale)
        made[1].append(dot_nt(refs.keep[place(0, n)], d_scores))
        made[2].append(dot_nt(d_context, raw))
        if n % per_block == per_block - 1:
            block = n // per_block
            for which in range(3):
                column = (which * blocks + block) * length
                whole = jnp.concatenate(made[which], axis=0).astype(bf16)
                refs.keep[rows, column : column + length] = whole.T
                made[which].clear()
            column = (3 * blocks + block) * length
            refs.keep[rows, column : column + length] = refs.keep[rows, column : column + length].T

    current = first(0)
    held = None
    for n in range(HEADS):
        j, place_in = n // per_block, n % per_block
        if place_in == 1 and j + 1 < blocks:
            unmix(j + 1)
        following = first(n + 1) if n + 1 < HEADS else None
        ready = second(n, *current)
        if held is not None:
            third(n - 1, *held)
        if place_in == 2 and j > 0:
            total = total + unproject(j - 1)
        held, current = ready, following
    third(HEADS - 1, *held)
    d_in = total + unproject(blocks - 1)
    refs.d_in[rows, :] = d_in.astype(bf16)


class Refs:
    def __init__(self, **named):
        self.__dict__.update(named)


def pipeline(
    sections,
    levels,
    tokens,
    cotangent,
    segments_in,
    weight_in,
    down_in,
    gain_in,
    shift_in,
    layer_out,
    input_out,
    first_out,
    down_out,
    norm_out,
    rows_in,
    keep,
    wide,
    grad,
    normal,
    scale,
    out,
    d_in,
    weight,
    down,
    norm_sums,
    d_context,
    inverse,
    segments,
    gains,
    load_sem,
    first_sem,
    forward_send,
    forward_recv,
    backward_send,
    backward_recv,
    share_send,
    share_recv,
    store_sem,
    stage=None,
    level_recv=None,
    norm_recv=None,
    norm_send=None,
    ready_sem=None,
    pair_sems=None,
    level_sems=None,
    norm_sems=None,
):
    dp = lax.axis_index("dp")
    section = lax.axis_index("section")
    batches, length = segments.shape
    width, hidden = weight.shape
    share = batches // sections
    final = sections - 1
    refs = Refs(
        rows_in=rows_in, keep=keep, wide=wide, grad=grad, normal=normal, scale=scale, out=out, d_in=d_in,
        weight=weight, down=down, norm_sums=norm_sums, d_context=d_context, inverse=inverse, segments=segments,
    )
    is_attention = lax.rem(section, 2) == 0
    is_feed = lax.rem(section, 2) == 1

    def load_rows(source, target, i):
        rows = aligned(i, length)
        return pltpu.make_async_copy(source.at[rows, :], target.at[rows, :], first_sem.at[i])

    def load_weight(part):
        columns = slice(part * width, (part + 1) * width)
        return pltpu.make_async_copy(weight_in.at[0, :, columns], weight.at[:, columns], load_sem.at[part])

    units = hidden // width
    load_down = pltpu.make_async_copy(down_in.at[0], down, load_sem.at[units])
    small = [
        pltpu.make_async_copy(source, target, load_sem.at[units + 1 + i])
        for i, (source, target) in enumerate(
            ((segments_in, segments), (gain_in, gains.at[0]), (shift_in, gains.at[1]))
        )
    ]
    load_weight(0).start()
    for copy in small:
        copy.start()
    for part in range(1, units):
        load_weight(part).start()

    @pl.when(is_feed)
    def _():
        load_down.start()

    @pl.when(section == 0)
    def _():
        for i in range(batches):
            load_rows(tokens, rows_in, i).start()

    @pl.when(section == final)
    def _():
        for i in range(batches):
            load_rows(cotangent, grad, i).start()

    barrier = pltpu.get_barrier_semaphore()
    for other in range(1, sections):
        pl.semaphore_signal(
            barrier, inc=1, device_id=(dp, lax.rem(section + other, sections)), device_id_type=MESH
        )
    if levels:
        pair, level = lax.rem(dp, 2), dp // 2
        partner = dp + 1 - 2 * pair
        pl.semaphore_signal(barrier, inc=1, device_id=(partner, section), device_id_type=MESH)
        peers = [lax.rem(dp + 2 * other, 2 * levels) for other in range(1, levels)]
        for peer in peers:
            pl.semaphore_signal(barrier, inc=1, device_id=(peer, section), device_id_type=MESH)
    norm_sums[...] = jnp.zeros_like(norm_sums)
    for copy in small:
        copy.wait()
    gain = gains[0]
    shift = gains[1]

    def meet():
        pl.semaphore_wait(barrier, sections - 1 + levels)

    def forward_copy(i):
        rows = aligned(i, length)
        return pltpu.make_async_remote_copy(
            out.at[rows, :], rows_in.at[rows, :], forward_send.at[i], forward_recv.at[i],
            device_id=(dp, lax.rem(section + 1, sections)), device_id_type=MESH,
        )

    def backward_copy(i):
        rows = aligned(i, length)
        return pltpu.make_async_remote_copy(
            d_in.at[rows, :], grad.at[rows, :], backward_send.at[i], backward_recv.at[i],
            device_id=(dp, lax.rem(section + sections - 1, sections)), device_id_type=MESH,
        )

    def share_copy(source, target, i, away):
        owner = i // share
        remote = pltpu.make_async_remote_copy(
            source.at[aligned(i, length), :], target.at[aligned(lax.rem(i, share), length), :],
            share_send.at[away, i], share_recv.at[away, lax.rem(i, share)],
            device_id=(dp, owner), device_id_type=MESH,
        )
        local = pltpu.make_async_copy(
            source.at[aligned(i, length), :], target.at[aligned(lax.rem(i, share), length), :],
            share_recv.at[away, lax.rem(i, share)],
        )
        return owner, remote, local

    def send_share(source, target, i, away):
        owner, remote, local = share_copy(source, target, i, away)

        @pl.when(owner == section)
        def _():
            local.start()

        @pl.when(owner != section)
        def _():
            remote.start()

    def before_forward(i):
        @pl.when(section == 0)
        def _():
            load_rows(tokens, rows_in, i).wait()

        @pl.when(section > 0)
        def _():
            forward_copy(i).wait_recv()

    def after_forward(i):
        @pl.when(section < final)
        def _():
            forward_copy(i).start()

    def before_backward(i):
        @pl.when(section == final)
        def _():
            load_rows(cotangent, grad, i).wait()

        @pl.when(section < final)
        def _():
            backward_copy(i).wait_recv()

    def after_backward(i):
        @pl.when(section > 0)
        def _():
            backward_copy(i).start()

        @pl.when(section == 0)
        def _():
            send_share(d_in, input_out, i, 1)

    lag = jnp.where(section == final, 0, jnp.where(section == final - 1, min(2, batches), batches))

    mask = (1 << (batches - 1).bit_length()) - 1

    def ticks(forward, backward):
        def tick(t, carry):
            @pl.when(t < batches)
            def _():
                i = t & mask
                before_forward(i)
                forward(i)
                after_forward(i)

            late = t - lag

            @pl.when((late >= 0) & (late < batches))
            def _():
                i = late & mask
                before_backward(i)
                backward(i)
                after_backward(i)

            return carry

        lax.fori_loop(0, 2 * batches, tick, 0)

    units = hidden // width

    def gradient_rows_left():
        @pl.when(section > 0)
        def _():
            def one(i, carry):
                backward_copy(i).wait_send()
                return carry

            lax.fori_loop(0, batches, one, 0)

    def send_output():
        @pl.when(section == final)
        def _():
            def one(i, carry):
                send_share(out, layer_out, i, 0)
                return carry

            lax.fori_loop(0, batches, one, 0)

    def drain():
        def one(i, carry):
            @pl.when(section < final)
            def _():
                forward_copy(i).wait_send()

            @pl.when((section > 0) & is_attention)
            def _():
                backward_copy(i).wait_send()

            for away, source, target, sender in ((0, out, layer_out, final), (1, d_in, input_out, 0)):
                owner, remote, local = share_copy(source, target, i, away)

                @pl.when((section == sender) & (owner != section))
                def _():
                    remote.wait_send()

                @pl.when((section == sender) & (owner == section))
                def _():
                    local.wait()

                @pl.when((section != sender) & (owner == section))
                def _():
                    remote.wait_recv()

            return carry

        lax.fori_loop(0, batches, one, 0)

    def plain_gradients(parts, late, line_first=()):
        def store(m, source, target, k):
            columns = aligned(k, width)
            return pltpu.make_async_copy(
                source.at[:, columns], target.at[:, columns], store_sem.at[m, k]
            )

        for m, (make, source, _, target) in enumerate(parts):

            def unit(k, carry):
                make(k, slice(0, width))
                store(m, source, target, k).start()
                return carry

            lax.fori_loop(0, units, unit, 0)
        send_output()
        norm_out[...] = jnp.sum(norm_sums[...], axis=1)
        for m, (make, source, _, target) in enumerate(parts):
            for k in range(units):
                store(m, source, target, k).wait()

    def summed_gradients(parts, late, line_first=()):
        columns_out = hidden // (2 * levels)
        halves = HALVES
        part_rows = width // halves

        above, below = levels - 1 - level, level

        def level_of(j):
            near_low = jnp.where(j < above, levels - 1 - j, j - above)
            near_high = jnp.where(j < below, j, levels - 1 - (j - below))
            moving = jnp.where(level < levels // 2, near_low, near_high)
            return jnp.where(j == levels - 1, level, moving)

        def half_of(source, k, side, h):
            column = pl.multiple_of(k * width + side * columns_out, columns_out)
            return source.at[pl.ds(h * part_rows, part_rows), pl.ds(column, columns_out)]

        def pair_slot(landing, k, h):
            row = pl.multiple_of((k // 2) * width + h * part_rows, part_rows)
            column = pl.multiple_of(lax.rem(k, 2) * columns_out, columns_out)
            return landing.at[pl.ds(row, part_rows), pl.ds(column, columns_out)]

        def pair_copy(m, k, h):
            _, source, landing, _ = parts[m]
            return pltpu.make_async_remote_copy(
                half_of(source, k, 1 - pair, h), pair_slot(landing, k, h),
                pair_sems.at[0, m, k, h], pair_sems.at[1, m, k, h],
                device_id=(partner, section), device_id_type=MESH,
            )

        def level_slot(m, slot, h):
            return level_recv.at[m, slot, pl.ds(h * part_rows, part_rows), :]

        def level_copy(m, k, h, other=False):
            step = jnp.where(k > level, 1, -1)
            slot = jnp.where(k == level - 1, levels, k)
            side = 1 - pair if other else pair
            place = 1 if other else m
            return pltpu.make_async_remote_copy(
                half_of(parts[m][1], k, side, h), level_slot(place, slot, h),
                level_sems.at[0, place, k, h], level_sems.at[1, place, slot, h],
                device_id=(dp + 2 * step, section), device_id_type=MESH,
            )

        def arrival(m, slot, h):
            return pltpu.make_async_copy(
                level_slot(m, slot, h), level_slot(m, slot, h), level_sems.at[1, m, slot, h]
            )

        def send_pair(m, k, some):
            for h in some:
                if h not in line_first:
                    pair_copy(m, k, h).start()

        def make_unit(m, k, t):
            for g in range(2):
                parts[m][0](k, slice(g * width // 2, (g + 1) * width // 2))
                if not line_first:
                    if g == 0:

                        @pl.when(lax.rem(t, units) == 0)
                        def _():
                            pl.semaphore_wait(ready_sem.at[m], 1)

                    send_pair(m, k, range(g * halves // 2, (g + 1) * halves // 2))

        def pass_on(m, k, h, mine, total, other=False):
            from_below = (k > level) & (level > 0)
            from_above = (k < level) & (level < levels - 1)
            moving = from_below | from_above
            place = 1 if other else m

            @pl.when(moving)
            def _():
                arrival(place, k, h).wait()
                mine[...] = (total() + level_slot(place, k, h)[...].astype(f32)).astype(bf16)

            @pl.when(jnp.logical_not(moving))
            def _():
                mine[...] = total().astype(bf16)

            @pl.when(k != level)
            def _():
                level_copy(m, k, h, other).start()

        def pass_line(m, k, t):
            source = parts[m][1]
            for h in line_first:

                @pl.when(k != level)
                def _():
                    for other in (False, True):
                        mine = half_of(source, k, 1 - pair if other else pair, h)
                        pass_on(m, k, h, mine, lambda: mine[...].astype(f32), other)

        def pass_pair(m, k, t):
            _, source, landing, _ = parts[m]
            for h in range(halves):
                if h in line_first:
                    continue
                pair_copy(m, k, h).wait_recv()
                mine = half_of(source, k, pair, h)
                theirs = pair_slot(landing, k, h)
                pass_on(m, k, h, mine, lambda: mine[...].astype(f32) + theirs[...].astype(f32))

        def gather(m, h, other=False):
            place = 1 if other else m
            side = 1 - pair if other else pair
            wanted = stage.at[pl.ds(h * part_rows, part_rows), :]
            wanted[...] = half_of(parts[m][1], level, side, h)[...].astype(f32)
            for there, slot in ((level > 0, level), (level < levels - 1, levels)):

                @pl.when(there)
                def _():
                    arrival(place, slot, h).wait()
                    wanted[...] += level_slot(place, slot, h)[...].astype(f32)

            return wanted

        def last_line(m):
            for h in line_first:
                half_of(parts[m][1], level, 1 - pair, h)[...] = gather(m, h, True)[...].astype(bf16)
                pair_copy(m, level, h).start()

        def last_unit(m):
            _, source, landing, target = parts[m]
            copies = []
            for h in [h for h in range(halves) if h not in line_first] + list(line_first):
                wanted = gather(m, h)
                if h in line_first:
                    pair_copy(m, level, h).wait_recv()
                    wanted[...] += pair_slot(landing, level, h)[...].astype(f32)
                rows = pl.ds(h * part_rows, part_rows)
                copies.append(pltpu.make_async_copy(wanted, target.at[0, rows, :], store_sem.at[m, h]))
                copies[-1].start()
            for copy in copies:
                copy.wait()

        def norm_copy(way, device):
            return pltpu.make_async_remote_copy(
                norm_send.at[min(way, 1)], norm_recv.at[way], norm_sems.at[0, way], norm_sems.at[1, way],
                device_id=(device, section), device_id_type=MESH,
            )

        def start_norms():
            norm_send[0] = jnp.concatenate(
                [jnp.sum(norm_sums[...], axis=1), jnp.zeros((6, width), f32)], axis=0
            )
            norm_copy(0, partner).start()

        def spread_norms():
            norm_copy(0, partner).wait_recv()
            norm_send[1] = norm_send[0] + norm_recv[0]
            for way, peer in enumerate(peers, 1):
                norm_copy(way, peer).start()

        def finish_norms():
            total = norm_send[1]
            for way, peer in enumerate(peers, 1):
                norm_copy(way, peer).wait_recv()
                total = total + norm_recv[way]
            norm_out[...] = total
            norm_copy(0, partner).wait_send()
            for way, peer in enumerate(peers, 1):
                norm_copy(way, peer).wait_send()

        def say_ready(m):
            pl.semaphore_signal(
                ready_sem.at[m], inc=1, device_id=(partner, section), device_id_type=MESH
            )

        say_ready(0)
        start_norms()
        total_units = len(parts) * units

        def of_unit(t, act):
            for m in range(len(parts)):

                @pl.when(t // units == m)
                def _():
                    act(m, level_of(lax.rem(t, units)), t)

        def turn(t, carry):
            @pl.when(t < total_units)
            def _():
                of_unit(t, make_unit)

            @pl.when(t == 0)
            def _():
                spread_norms()
                if len(parts) > 1:
                    gradient_rows_left()
                    say_ready(1)

            if len(parts) > 1:

                @pl.when(t == total_units + late - 1)
                def _():
                    last_unit(0)

            @pl.when(t >= late)
            def _():
                of_unit(t - late, pass_line if line_first else pass_pair)

            return carry

        lax.fori_loop(0, total_units, turn, 0)
        send_output()
        lax.fori_loop(total_units, total_units + late, turn, 0)
        if line_first:
            pl.semaphore_wait(ready_sem.at[0], 1)
            def start(j, carry):
                send_pair(0, level_of(j), range(halves))
                return carry

            def end(j, carry):
                pass_pair(0, level_of(j), j)
                return carry

            lax.fori_loop(0, units, start, 0)
            last_line(0)
            lax.fori_loop(0, units, end, 0)
        last_unit(len(parts) - 1)
        finish_norms()

        def sent(k, carry):
            for m in range(len(parts)):
                for h in range(halves):
                    if h not in line_first:
                        pair_copy(m, k, h).wait_send()

                    @pl.when(k != level)
                    def _():
                        level_copy(m, k, h).wait_send()
                        if h in line_first:
                            level_copy(m, k, h, True).wait_send()

            return carry

        lax.fori_loop(0, units, sent, 0)
        for m in range(len(parts)):
            for h in line_first:
                pair_copy(m, level, h).wait_send()

    weight_gradients = summed_gradients if levels else plain_gradients

    @pl.when(is_attention)
    def _():
        for which in range(3):
            columns = slice(which * width, (which + 1) * width)
            load_weight(which).wait()
            down[:, columns] = weight[:, columns].T
        for part in range(3, units):
            load_weight(part).wait()
        meet()
        ticks(
            lambda i: attend_forward(i, gain, shift, refs),
            lambda i: attend_backward(i, gain, refs),
        )

        def first(k, some):
            columns = aligned(k, width)

            @pl.when(k < units - 1)
            def _():
                weight[some, columns] = dot_tn(rows_in[:, some], keep[:, columns]).astype(bf16)

            @pl.when(k == units - 1)
            def _():
                context = keep[:, 3 * width + some.start : 3 * width + some.stop]
                weight[some, columns] = dot_tn(context, grad[...]).astype(bf16)

        weight_gradients(((first, weight, normal, first_out),), 1, (0,))

    @pl.when(is_feed)
    def _():
        for part in range(units):
            load_weight(part).wait()
        load_down.wait()
        meet()
        ticks(
            lambda i: feed_forward(aligned(i, length), gain, shift, refs),
            lambda i: feed_backward(aligned(i, length), gain, refs),
        )

        def first(k, some):
            columns = aligned(k, width)
            weight[some, columns] = dot_tn(rows_in[:, some], wide[:, columns]).astype(bf16)

        def second(k, some):
            columns = aligned(k, width)
            down[some, columns] = dot_tn(grad[:, some], keep[:, columns]).astype(bf16)

        weight_gradients(
            ((first, weight, normal, first_out), (second, down, d_in, down_out)), 3
        )

    drain()


def hand_over(*refs):
    sources, norms, targets, (gain_out, shift_out) = refs[:4], refs[4], refs[5:9], refs[9:11]
    held, sems = refs[11:15], refs[15]
    has_down = lax.rem(lax.axis_index("section"), 2) == 1
    fetch = [pltpu.make_async_copy(sources[i], held[i], sems.at[0, i]) for i in range(4)]
    store = [pltpu.make_async_copy(held[i], targets[i], sems.at[1, i]) for i in range(4)]
    for i in range(3):
        fetch[i].start()

    @pl.when(has_down)
    def _():
        fetch[3].start()

    @pl.when(jnp.logical_not(has_down))
    def _():
        held[3][...] = jnp.zeros_like(held[3])
        store[3].start()

    width, own = norms.shape[1], gain_out.shape[1]
    turned = pltpu.roll(norms[...], lax.rem(width - lax.axis_index("dp") * own, width), 1)
    gain_out[...] = turned[0:1, :own]
    shift_out[...] = turned[1:2, :own]
    for i in range(3):
        fetch[i].wait()
        store[i].start()

    @pl.when(has_down)
    def _():
        fetch[3].wait()
        store[3].start()

    for i in range(4):
        store[i].wait()


def on_device(tokens, cotangent, segment_ids, first_weight, down_weight, ln_gain, ln_shift):
    sections = lax.axis_size("section")
    groups = lax.axis_size("dp")
    count, width = tokens.shape
    batches, length = segment_ids.shape
    hidden = first_weight.shape[2]
    units = hidden // width
    share = batches // sections
    levels = units if groups == 2 * units and (units + 1) // 2 * width <= count else 0
    columns_out = hidden // groups
    any_space = pl.BlockSpec(memory_space=pl.ANY)
    vmem = pl.BlockSpec(memory_space=pltpu.VMEM)
    dma = pltpu.SemaphoreType.DMA
    if levels:
        sums = [jax.ShapeDtypeStruct((1, width, columns_out), f32)] * 2
        sums.append(jax.ShapeDtypeStruct((8, width), f32))
    else:
        sums = [jax.ShapeDtypeStruct((width, hidden), bf16)] * 2
        sums.append(jax.ShapeDtypeStruct((2, width), f32))
    scratch = [
        pltpu.VMEM((count, width), bf16),
        pltpu.VMEM((count, hidden), bf16),
        pltpu.VMEM((count, hidden), bf16),
        pltpu.VMEM((count, width), bf16),
        pltpu.VMEM((count, width), bf16),
        pltpu.VMEM((count, 1), f32),
        pltpu.VMEM((count, width), bf16),
        pltpu.VMEM((count, width), bf16),
        pltpu.VMEM((width, hidden), bf16),
        pltpu.VMEM((width, hidden), bf16),
        pltpu.VMEM((2, 8, width), f32),
        pltpu.VMEM((width, length), f32),
        pltpu.VMEM((batches * 16, length), f32),
        pltpu.VMEM((batches, length), jnp.int32),
        pltpu.VMEM((2, 1, width), f32),
        dma((units + 4,)),
        dma((batches,)),
        dma((batches,)),
        dma((batches,)),
        dma((batches,)),
        dma((batches,)),
        dma((2, batches)),
        dma((2, share)),
        dma((2, units)),
    ]
    if levels:
        scratch += [
            pltpu.VMEM((width, columns_out), f32),
            pltpu.VMEM((2, levels + 1, width, columns_out), bf16),
            pltpu.VMEM((levels, 8, width), f32),
            pltpu.VMEM((2, 8, width), f32),
            pltpu.SemaphoreType.REGULAR((2,)),
            dma((2, 2, levels, HALVES)),
            dma((2, 2, levels + 1, HALVES)),
            dma((2, levels)),
        ]
    results = pl.pallas_call(
        functools.partial(pipeline, sections, levels),
        out_shape=(
            jax.ShapeDtypeStruct((count // sections, width), bf16),
            jax.ShapeDtypeStruct((count // sections, width), bf16),
            *sums,
        ),
        in_specs=[any_space] * 7,
        out_specs=(any_space, any_space, any_space, any_space, vmem),
        scratch_shapes=scratch,
        compiler_params=pltpu.CompilerParams(
            collective_id=0, has_side_effects=True, vmem_limit_bytes=64 * 2**20
        ),
    )(tokens, cotangent, segment_ids, first_weight, down_weight, ln_gain, ln_shift)
    if levels:
        own = jax.ShapeDtypeStruct((1, width // groups), f32)
        return pl.pallas_call(
            hand_over,
            out_shape=tuple(jax.ShapeDtypeStruct(r.shape, r.dtype) for r in results[:4]) + (own, own),
            in_specs=[any_space] * 4 + [vmem],
            out_specs=(any_space,) * 4 + (vmem,) * 2,
            scratch_shapes=[pltpu.VMEM(r.shape, r.dtype) for r in results[:4]] + [dma((2, 4))],
        )(*results)
    layer_rows, input_rows, first_sum, down_sum, norm_sum = results
    has_down = lax.rem(lax.axis_index("section"), 2) == 1
    down_sum = jnp.where(has_down, down_sum, jnp.zeros_like(down_sum))
    first_sum, down_sum, norm_sum = (
        lax.psum_scatter(value, "dp", scatter_dimension=1, tiled=True)
        for value in (first_sum, down_sum, norm_sum)
    )
    first_sum, down_sum = first_sum.astype(f32)[None], down_sum.astype(f32)[None]
    return (layer_rows, input_rows, first_sum, down_sum, norm_sum[0:1], norm_sum[1:2])


def solution(mesh):
    return jax.shard_map(
        on_device,
        mesh=mesh,
        in_specs=(
            P("dp", None),
            P("dp", None),
            P("dp", None),
            P("section", None, None),
            P("section", None, None),
            P("section", None),
            P("section", None),
        ),
        out_specs=(
            P(("dp", "section"), None),
            P(("dp", "section"), None),
            P("section", None, "dp"),
            P("section", None, "dp"),
            P("section", "dp"),
            P("section", "dp"),
        ),
        check_vma=False,
    )
```

```python
import functools

import jax
import jax.numpy as jnp
from jax import lax
from jax.experimental import pallas as pl
from jax.experimental.pallas import tpu as pltpu
from jax.sharding import PartitionSpec as P

HEADS = 12
HALVES = 4
NORM_EPSILON = 1e-12
MASKED_SCORE = -1e30
INV_SQRT2 = 0.7071067811865476
INV_SQRT2PI = 0.3989422804014327
MESH = pl.DeviceIdType.MESH
bf16 = jnp.bfloat16
f32 = jnp.float32


def dot(a, b):
    return jnp.dot(a, b, preferred_element_type=f32)


def dot_nt(a, b):
    return lax.dot_general(a, b, (((1,), (1,)), ((), ())), preferred_element_type=f32)


def dot_tn(a, b):
    return lax.dot_general(a, b, (((0,), (0,)), ((), ())), preferred_element_type=f32)


def aligned(index, size):
    return pl.ds(pl.multiple_of(index * size, size), size)


def norm_forward(residual, rows, gain, shift, refs):
    mean = jnp.mean(residual, axis=-1, keepdims=True)
    centered = residual - mean
    spread = jnp.mean(centered * centered, axis=-1, keepdims=True)
    scale = lax.rsqrt(spread + NORM_EPSILON)
    normal = centered * scale
    refs.normal[rows, :] = normal.astype(bf16)
    refs.scale[rows, :] = scale
    refs.out[rows, :] = (normal * gain + shift).astype(bf16)


def norm_backward(rows, gain, refs):
    upstream = refs.grad[rows, :].astype(f32)
    normal = refs.normal[rows, :].astype(f32)
    scale = refs.scale[rows, :]
    count, width = upstream.shape
    refs.norm_sums[0] += jnp.sum((upstream * normal).reshape(count // 8, 8, width), axis=0)
    refs.norm_sums[1] += jnp.sum(upstream.reshape(count // 8, 8, width), axis=0)
    pulled = upstream * gain
    mean = jnp.mean(pulled, axis=-1, keepdims=True)
    along = jnp.mean(pulled * normal, axis=-1, keepdims=True)
    d_resid = scale * (pulled - mean - normal * along)
    refs.grad[rows, :] = d_resid.astype(bf16)
    return d_resid


def feed_forward(rows, gain, shift, refs):
    width, hidden = refs.weight.shape
    tile = width
    tiles = hidden // tile
    source = refs.rows_in[rows, :]
    residual = source.astype(f32)

    def up(t):
        return dot(source, refs.weight[:, t * tile : (t + 1) * tile])

    def down(value, t):
        return dot_nt(value, refs.down[:, t * tile : (t + 1) * tile])

    pre = up(0)
    held = None
    for t in range(tiles):
        following = up(t + 1) if t + 1 < tiles else None
        cdf = 0.5 + 0.5 * lax.erf(pre * INV_SQRT2)
        value = (pre * cdf).astype(bf16)
        slope = cdf + pre * (INV_SQRT2PI * jnp.exp(-0.5 * pre * pre))
        refs.keep[rows, t * tile : (t + 1) * tile] = value
        refs.wide[rows, t * tile : (t + 1) * tile] = slope.astype(bf16)
        if held is not None:
            residual = residual + down(held, t - 1)
        held, pre = value, following
    residual = residual + down(held, tiles - 1)
    norm_forward(residual, rows, gain, shift, refs)


def feed_backward(rows, gain, refs):
    width, hidden = refs.weight.shape
    tile = width
    tiles = hidden // tile
    d_resid = norm_backward(rows, gain, refs)
    d_branch = d_resid.astype(bf16)
    total = d_resid

    def up(t):
        return dot(d_branch, refs.down[:, t * tile : (t + 1) * tile])

    def down(value, t):
        return dot_nt(value, refs.weight[:, t * tile : (t + 1) * tile])

    d_hidden = up(0)
    held = None
    for t in range(tiles):
        following = up(t + 1) if t + 1 < tiles else None
        columns = slice(t * tile, (t + 1) * tile)
        d_pre = (d_hidden * refs.wide[rows, columns].astype(f32)).astype(bf16)
        refs.wide[rows, columns] = d_pre
        if held is not None:
            total = total + down(held, t - 1)
        held, d_hidden = d_pre, following
    total = total + down(held, tiles - 1)
    refs.d_in[rows, :] = total.astype(bf16)


def head_part(refs, first_row, length, blocks, which, n):
    head_width = refs.weight.shape[0] // HEADS
    per_block = length // head_width
    column = (which * blocks + n // per_block) * length
    rows = pl.ds(pl.multiple_of(first_row + (n % per_block) * head_width, head_width), head_width)
    return rows, slice(column, column + length)


def attend_forward(index, gain, shift, refs):
    length = refs.segments.shape[1]
    width = refs.weight.shape[0]
    blocks = width // length
    rows = aligned(index, length)
    first_row = index * length
    source = refs.rows_in[rows, :]
    ids = jnp.broadcast_to(refs.segments[pl.ds(index, 1), :].astype(f32), (length, length))
    allowed = ids == ids.T
    score_scale = (width // HEADS) ** (-0.5)
    for which in range(3):
        turned = dot_nt(refs.down[:, which * width : (which + 1) * width], source)
        if which == 0:
            turned = turned * score_scale
        turned = turned.astype(bf16)
        for j in range(blocks):
            column = (which * blocks + j) * length
            refs.keep[rows, column : column + length] = turned[j * length : (j + 1) * length, :]
    place = functools.partial(head_part, refs, first_row, length, blocks)

    def score(n):
        return dot_tn(refs.keep[place(1, n)], refs.keep[place(0, n)])

    def weigh(scores):
        scores = jnp.where(allowed, scores, MASKED_SCORE)
        raw = jnp.exp(scores - jnp.max(scores, axis=0, keepdims=True))
        return raw.astype(bf16), 1.0 / jnp.sum(raw, axis=0, keepdims=True)

    def finish(n, raw, inverse):
        refs.wide[rows, n * length : (n + 1) * length] = raw
        refs.inverse[pl.ds(index * 16 + n, 1), :] = inverse
        refs.keep[place(3, n)] = (dot(refs.keep[place(2, n)], raw) * inverse).astype(bf16)

    ahead = 3
    scores = [score(n) for n in range(ahead)]
    held = None
    for n in range(HEADS):
        if n + ahead < HEADS:
            scores.append(score(n + ahead))
        current = weigh(scores[n])
        if held is not None:
            finish(n - 1, *held)
        held = current
    finish(HEADS - 1, *held)
    residual = source.astype(f32)
    for j in range(blocks):
        column = (3 * blocks + j) * length
        residual = residual + dot_tn(
            refs.keep[rows, column : column + length],
            refs.weight[j * length : (j + 1) * length, 3 * width :],
        )
    norm_forward(residual, rows, gain, shift, refs)


def attend_backward(index, gain, refs):
    length = refs.segments.shape[1]
    width = refs.weight.shape[0]
    head_width = width // HEADS
    blocks = width // length
    per_block = length // head_width
    score_scale = head_width ** (-0.5)
    rows = aligned(index, length)
    first_row = index * length
    d_resid = norm_backward(rows, gain, refs)
    d_branch = d_resid.astype(bf16)
    total = d_resid

    def unmix(j):
        some = slice(j * length, (j + 1) * length)
        refs.d_context[some, :] = dot_nt(refs.weight[some, 3 * width :], d_branch)

    def unproject(j):
        some = [slice((which * blocks + j) * length, (which * blocks + j + 1) * length) for which in range(3)]
        left = jnp.concatenate([refs.keep[rows, part] for part in some], axis=1)
        right = jnp.concatenate([refs.weight[:, part] for part in some], axis=1)
        return dot_nt(left, right)

    unmix(0)
    place = functools.partial(head_part, refs, first_row, length, blocks)

    def first(n):
        inverse = refs.inverse[pl.ds(index * 16 + n, 1), :]
        d_context = refs.d_context[n * head_width : (n + 1) * head_width, :] * inverse
        along = jnp.sum(d_context * refs.keep[place(3, n)].astype(f32), axis=0, keepdims=True)
        d_context = d_context.astype(bf16)
        return dot_tn(refs.keep[place(2, n)], d_context), along, d_context

    def second(n, d_probs, along, d_context):
        raw = refs.wide[rows, n * length : (n + 1) * length]
        return (raw.astype(f32) * (d_probs - along)).astype(bf16), raw, d_context

    made = ([], [], [])

    def third(n, d_scores, raw, d_context):
        made[0].append(dot(refs.keep[place(1, n)], d_scores) * score_scale)
        made[1].append(dot_nt(refs.keep[place(0, n)], d_scores))
        made[2].append(dot_nt(d_context, raw))
        if n % per_block == per_block - 1:
            block = n // per_block
            for which in range(3):
                column = (which * blocks + block) * length
                whole = jnp.concatenate(made[which], axis=0).astype(bf16)
                refs.keep[rows, column : column + length] = whole.T
                made[which].clear()
            column = (3 * blocks + block) * length
            refs.keep[rows, column : column + length] = refs.keep[rows, column : column + length].T

    current = first(0)
    held = None
    for n in range(HEADS):
        j, place_in = n // per_block, n % per_block
        if place_in == 1 and j + 1 < blocks:
            unmix(j + 1)
        following = first(n + 1) if n + 1 < HEADS else None
        ready = second(n, *current)
        if held is not None:
            third(n - 1, *held)
        if place_in == 2 and j > 0:
            total = total + unproject(j - 1)
        held, current = ready, following
    third(HEADS - 1, *held)
    d_in = total + unproject(blocks - 1)
    refs.d_in[rows, :] = d_in.astype(bf16)


class Refs:
    def __init__(self, **named):
        self.__dict__.update(named)


def pipeline(
    sections,
    levels,
    tokens,
    cotangent,
    segments_in,
    weight_in,
    down_in,
    gain_in,
    shift_in,
    layer_out,
    input_out,
    first_out,
    down_out,
    norm_out,
    rows_in,
    keep,
    wide,
    grad,
    normal,
    scale,
    out,
    d_in,
    weight,
    down,
    norm_sums,
    d_context,
    inverse,
    segments,
    gains,
    load_sem,
    first_sem,
    forward_send,
    forward_recv,
    backward_send,
    backward_recv,
    share_send,
    share_recv,
    store_sem,
    stage=None,
    level_recv=None,
    norm_recv=None,
    norm_send=None,
    ready_sem=None,
    pair_sems=None,
    level_sems=None,
    norm_sems=None,
):
    dp = lax.axis_index("dp")
    section = lax.axis_index("section")
    batches, length = segments.shape
    width, hidden = weight.shape
    share = batches // sections
    final = sections - 1
    refs = Refs(
        rows_in=rows_in, keep=keep, wide=wide, grad=grad, normal=normal, scale=scale, out=out, d_in=d_in,
        weight=weight, down=down, norm_sums=norm_sums, d_context=d_context, inverse=inverse, segments=segments,
    )
    is_attention = lax.rem(section, 2) == 0
    is_feed = lax.rem(section, 2) == 1

    def load_rows(source, target, i):
        rows = aligned(i, length)
        return pltpu.make_async_copy(source.at[rows, :], target.at[rows, :], first_sem.at[i])

    def load_weight(part):
        columns = slice(part * width, (part + 1) * width)
        return pltpu.make_async_copy(weight_in.at[0, :, columns], weight.at[:, columns], load_sem.at[part])

    units = hidden // width
    load_down = pltpu.make_async_copy(down_in.at[0], down, load_sem.at[units])
    small = [
        pltpu.make_async_copy(source, target, load_sem.at[units + 1 + i])
        for i, (source, target) in enumerate(
            ((segments_in, segments), (gain_in, gains.at[0]), (shift_in, gains.at[1]))
        )
    ]
    load_weight(0).start()
    for copy in small:
        copy.start()

    @pl.when(section == 0)
    def _():
        load_rows(tokens, rows_in, 0).start()

    for part in range(1, units):
        load_weight(part).start()

    @pl.when(is_feed)
    def _():
        load_down.start()

    @pl.when(section == 0)
    def _():
        for i in range(1, batches):
            load_rows(tokens, rows_in, i).start()

    @pl.when(section == final)
    def _():
        for i in range(batches):
            load_rows(cotangent, grad, i).start()

    barrier = pltpu.get_barrier_semaphore()
    for other in range(1, sections):
        pl.semaphore_signal(
            barrier, inc=1, device_id=(dp, lax.rem(section + other, sections)), device_id_type=MESH
        )
    if levels:
        pair, level = lax.rem(dp, 2), dp // 2
        partner = dp + 1 - 2 * pair
        pl.semaphore_signal(barrier, inc=1, device_id=(partner, section), device_id_type=MESH)
        peers = [lax.rem(dp + 2 * other, 2 * levels) for other in range(1, levels)]
        for peer in peers:
            pl.semaphore_signal(barrier, inc=1, device_id=(peer, section), device_id_type=MESH)
    norm_sums[...] = jnp.zeros_like(norm_sums)
    for copy in small:
        copy.wait()
    gain = gains[0]
    shift = gains[1]

    def meet():
        pl.semaphore_wait(barrier, sections - 1 + levels)

    def forward_copy(i):
        rows = aligned(i, length)
        return pltpu.make_async_remote_copy(
            out.at[rows, :], rows_in.at[rows, :], forward_send.at[i], forward_recv.at[i],
            device_id=(dp, lax.rem(section + 1, sections)), device_id_type=MESH,
        )

    def backward_copy(i):
        rows = aligned(i, length)
        return pltpu.make_async_remote_copy(
            d_in.at[rows, :], grad.at[rows, :], backward_send.at[i], backward_recv.at[i],
            device_id=(dp, lax.rem(section + sections - 1, sections)), device_id_type=MESH,
        )

    def share_copy(source, target, i, away):
        owner = i // share
        remote = pltpu.make_async_remote_copy(
            source.at[aligned(i, length), :], target.at[aligned(lax.rem(i, share), length), :],
            share_send.at[away, i], share_recv.at[away, lax.rem(i, share)],
            device_id=(dp, owner), device_id_type=MESH,
        )
        local = pltpu.make_async_copy(
            source.at[aligned(i, length), :], target.at[aligned(lax.rem(i, share), length), :],
            share_recv.at[away, lax.rem(i, share)],
        )
        return owner, remote, local

    def send_share(source, target, i, away):
        owner, remote, local = share_copy(source, target, i, away)

        @pl.when(owner == section)
        def _():
            local.start()

        @pl.when(owner != section)
        def _():
            remote.start()

    def before_forward(i):
        @pl.when(section == 0)
        def _():
            load_rows(tokens, rows_in, i).wait()

        @pl.when(section > 0)
        def _():
            forward_copy(i).wait_recv()

    def after_forward(i):
        @pl.when(section < final)
        def _():
            forward_copy(i).start()

    def before_backward(i):
        @pl.when(section == final)
        def _():
            load_rows(cotangent, grad, i).wait()

        @pl.when(section < final)
        def _():
            backward_copy(i).wait_recv()

    def after_backward(i):
        @pl.when(section > 0)
        def _():
            backward_copy(i).start()

        @pl.when(section == 0)
        def _():
            send_share(d_in, input_out, i, 1)

    lag = jnp.where(section == final, 0, jnp.where(section == final - 1, min(2, batches), batches))

    mask = (1 << (batches - 1).bit_length()) - 1

    def ticks(forward, backward):
        def tick(t, carry):
            @pl.when(t < batches)
            def _():
                i = t & mask
                before_forward(i)
                forward(i)
                after_forward(i)

            late = t - lag

            @pl.when((late >= 0) & (late < batches))
            def _():
                i = late & mask
                before_backward(i)
                backward(i)
                after_backward(i)

            return carry

        lax.fori_loop(0, 2 * batches, tick, 0)

    units = hidden // width

    def gradient_rows_left():
        @pl.when(section > 0)
        def _():
            def one(i, carry):
                backward_copy(i).wait_send()
                return carry

            lax.fori_loop(0, batches, one, 0)

    def send_output():
        @pl.when(section == final)
        def _():
            def one(i, carry):
                send_share(out, layer_out, i, 0)
                return carry

            lax.fori_loop(0, batches, one, 0)

    def drain():
        def one(i, carry):
            @pl.when(section < final)
            def _():
                forward_copy(i).wait_send()

            @pl.when((section > 0) & is_attention)
            def _():
                backward_copy(i).wait_send()

            for away, source, target, sender in ((0, out, layer_out, final), (1, d_in, input_out, 0)):
                owner, remote, local = share_copy(source, target, i, away)

                @pl.when((section == sender) & (owner != section))
                def _():
                    remote.wait_send()

                @pl.when((section == sender) & (owner == section))
                def _():
                    local.wait()

                @pl.when((section != sender) & (owner == section))
                def _():
                    remote.wait_recv()

            return carry

        lax.fori_loop(0, batches, one, 0)

    def plain_gradients(parts, late, line_first=()):
        def store(m, source, target, k):
            columns = aligned(k, width)
            return pltpu.make_async_copy(
                source.at[:, columns], target.at[:, columns], store_sem.at[m, k]
            )

        for m, (make, source, _, target) in enumerate(parts):

            def unit(k, carry):
                make(k, slice(0, width))
                store(m, source, target, k).start()
                return carry

            lax.fori_loop(0, units, unit, 0)
        send_output()
        if len(parts) > 1:
            gradient_rows_left()
        norm_out[...] = jnp.sum(norm_sums[...], axis=1)
        for m, (make, source, _, target) in enumerate(parts):
            for k in range(units):
                store(m, source, target, k).wait()

    def summed_gradients(parts, late, line_first=()):
        columns_out = hidden // (2 * levels)
        halves = HALVES
        part_rows = width // halves

        above, below = levels - 1 - level, level

        def level_of(j):
            near_low = jnp.where(j < above, levels - 1 - j, j - above)
            near_high = jnp.where(j < below, j, levels - 1 - (j - below))
            moving = jnp.where(level < levels // 2, near_low, near_high)
            return jnp.where(j == levels - 1, level, moving)

        def half_of(source, k, side, h):
            column = pl.multiple_of(k * width + side * columns_out, columns_out)
            return source.at[pl.ds(h * part_rows, part_rows), pl.ds(column, columns_out)]

        def pair_slot(landing, k, h):
            row = pl.multiple_of((k // 2) * width + h * part_rows, part_rows)
            column = pl.multiple_of(lax.rem(k, 2) * columns_out, columns_out)
            return landing.at[pl.ds(row, part_rows), pl.ds(column, columns_out)]

        def pair_copy(m, k, h):
            _, source, landing, _ = parts[m]
            return pltpu.make_async_remote_copy(
                half_of(source, k, 1 - pair, h), pair_slot(landing, k, h),
                pair_sems.at[0, m, k, h], pair_sems.at[1, m, k, h],
                device_id=(partner, section), device_id_type=MESH,
            )

        def level_slot(m, slot, h):
            return level_recv.at[m, slot, pl.ds(h * part_rows, part_rows), :]

        def level_copy(m, k, h, other=False):
            step = jnp.where(k > level, 1, -1)
            slot = jnp.where(k == level - 1, levels, k)
            side = 1 - pair if other else pair
            place = 1 if other else m
            return pltpu.make_async_remote_copy(
                half_of(parts[m][1], k, side, h), level_slot(place, slot, h),
                level_sems.at[0, place, k, h], level_sems.at[1, place, slot, h],
                device_id=(dp + 2 * step, section), device_id_type=MESH,
            )

        def arrival(m, slot, h):
            return pltpu.make_async_copy(
                level_slot(m, slot, h), level_slot(m, slot, h), level_sems.at[1, m, slot, h]
            )

        def send_pair(m, k, some):
            for h in some:
                if h not in line_first:
                    pair_copy(m, k, h).start()

        def make_unit(m, k, t):
            for g in range(2):
                parts[m][0](k, slice(g * width // 2, (g + 1) * width // 2))
                if not line_first:
                    if g == 0:

                        @pl.when(lax.rem(t, units) == 0)
                        def _():
                            pl.semaphore_wait(ready_sem.at[m], 1)

                    send_pair(m, k, range(g * halves // 2, (g + 1) * halves // 2))

        def pass_on(m, k, h, mine, total, other=False):
            from_below = (k > level) & (level > 0)
            from_above = (k < level) & (level < levels - 1)
            moving = from_below | from_above
            place = 1 if other else m

            @pl.when(moving)
            def _():
                arrival(place, k, h).wait()
                mine[...] = (total() + level_slot(place, k, h)[...].astype(f32)).astype(bf16)

            @pl.when(jnp.logical_not(moving))
            def _():
                mine[...] = total().astype(bf16)

            @pl.when(k != level)
            def _():
                level_copy(m, k, h, other).start()

        def pass_line(m, k, t):
            source = parts[m][1]
            for h in line_first:

                @pl.when(k != level)
                def _():
                    for other in (False, True):
                        mine = half_of(source, k, 1 - pair if other else pair, h)
                        pass_on(m, k, h, mine, lambda: mine[...].astype(f32), other)

        def pass_pair(m, k, t):
            _, source, landing, _ = parts[m]
            for h in range(halves):
                if h in line_first:
                    continue
                pair_copy(m, k, h).wait_recv()
                mine = half_of(source, k, pair, h)
                theirs = pair_slot(landing, k, h)
                pass_on(m, k, h, mine, lambda: mine[...].astype(f32) + theirs[...].astype(f32))

        def gather(m, h, other=False):
            place = 1 if other else m
            side = 1 - pair if other else pair
            wanted = stage.at[pl.ds(h * part_rows, part_rows), :]
            wanted[...] = half_of(parts[m][1], level, side, h)[...].astype(f32)
            for there, slot in ((level > 0, level), (level < levels - 1, levels)):

                @pl.when(there)
                def _():
                    arrival(place, slot, h).wait()
                    wanted[...] += level_slot(place, slot, h)[...].astype(f32)

            return wanted

        def last_line(m):
            for h in line_first:
                half_of(parts[m][1], level, 1 - pair, h)[...] = gather(m, h, True)[...].astype(bf16)
                pair_copy(m, level, h).start()

        def last_unit(m):
            _, source, landing, target = parts[m]
            copies = []
            for h in [h for h in range(halves) if h not in line_first] + list(line_first):
                wanted = gather(m, h)
                if h in line_first:
                    pair_copy(m, level, h).wait_recv()
                    wanted[...] += pair_slot(landing, level, h)[...].astype(f32)
                rows = pl.ds(h * part_rows, part_rows)
                copies.append(pltpu.make_async_copy(wanted, target.at[0, rows, :], store_sem.at[m, h]))
                copies[-1].start()
            for copy in copies:
                copy.wait()

        def norm_copy(way, device):
            return pltpu.make_async_remote_copy(
                norm_send.at[min(way, 1)], norm_recv.at[way], norm_sems.at[0, way], norm_sems.at[1, way],
                device_id=(device, section), device_id_type=MESH,
            )

        def start_norms():
            norm_send[0] = jnp.concatenate(
                [jnp.sum(norm_sums[...], axis=1), jnp.zeros((6, width), f32)], axis=0
            )
            norm_copy(0, partner).start()

        def spread_norms():
            norm_copy(0, partner).wait_recv()
            norm_send[1] = norm_send[0] + norm_recv[0]
            for way, peer in enumerate(peers, 1):
                norm_copy(way, peer).start()

        def finish_norms():
            total = norm_send[1]
            for way, peer in enumerate(peers, 1):
                norm_copy(way, peer).wait_recv()
                total = total + norm_recv[way]
            norm_out[...] = total
            norm_copy(0, partner).wait_send()
            for way, peer in enumerate(peers, 1):
                norm_copy(way, peer).wait_send()

        def say_ready(m):
            pl.semaphore_signal(
                ready_sem.at[m], inc=1, device_id=(partner, section), device_id_type=MESH
            )

        say_ready(0)
        start_norms()
        total_units = len(parts) * units

        def of_unit(t, act):
            for m in range(len(parts)):

                @pl.when(t // units == m)
                def _():
                    act(m, level_of(lax.rem(t, units)), t)

        def turn(t, carry):
            @pl.when(t < total_units)
            def _():
                of_unit(t, make_unit)

            @pl.when(t == 0)
            def _():
                spread_norms()
                if len(parts) > 1:
                    gradient_rows_left()
                    say_ready(1)

            if len(parts) > 1:

                @pl.when(t == total_units + late - 1)
                def _():
                    last_unit(0)

            @pl.when(t >= late)
            def _():
                of_unit(t - late, pass_line if line_first else pass_pair)

            return carry

        lax.fori_loop(0, total_units, turn, 0)
        send_output()
        lax.fori_loop(total_units, total_units + late, turn, 0)
        if line_first:
            pl.semaphore_wait(ready_sem.at[0], 1)
            def start(j, carry):
                send_pair(0, level_of(j), range(halves))
                return carry

            def end(j, carry):
                pass_pair(0, level_of(j), j)
                return carry

            lax.fori_loop(0, units, start, 0)
            last_line(0)
            lax.fori_loop(0, units, end, 0)
        last_unit(len(parts) - 1)
        finish_norms()

        def sent(k, carry):
            for m in range(len(parts)):
                for h in range(halves):
                    if h not in line_first:
                        pair_copy(m, k, h).wait_send()

                    @pl.when(k != level)
                    def _():
                        level_copy(m, k, h).wait_send()
                        if h in line_first:
                            level_copy(m, k, h, True).wait_send()

            return carry

        lax.fori_loop(0, units, sent, 0)
        for m in range(len(parts)):
            for h in line_first:
                pair_copy(m, level, h).wait_send()

    weight_gradients = summed_gradients if levels else plain_gradients

    @pl.when(is_attention)
    def _():
        for which in range(3):
            columns = slice(which * width, (which + 1) * width)
            load_weight(which).wait()
            down[:, columns] = weight[:, columns].T
        for part in range(3, units):
            load_weight(part).wait()
        meet()
        ticks(
            lambda i: attend_forward(i, gain, shift, refs),
            lambda i: attend_backward(i, gain, refs),
        )

        def first(k, some):
            columns = aligned(k, width)

            @pl.when(k < units - 1)
            def _():
                weight[some, columns] = dot_tn(rows_in[:, some], keep[:, columns]).astype(bf16)

            @pl.when(k == units - 1)
            def _():
                context = keep[:, 3 * width + some.start : 3 * width + some.stop]
                weight[some, columns] = dot_tn(context, grad[...]).astype(bf16)

        weight_gradients(((first, weight, normal, first_out),), 1, (0,))

    @pl.when(is_feed)
    def _():
        for part in range(units):
            load_weight(part).wait()
        load_down.wait()
        meet()
        ticks(
            lambda i: feed_forward(aligned(i, length), gain, shift, refs),
            lambda i: feed_backward(aligned(i, length), gain, refs),
        )

        def first(k, some):
            columns = aligned(k, width)
            weight[some, columns] = dot_tn(rows_in[:, some], wide[:, columns]).astype(bf16)

        def second(k, some):
            columns = aligned(k, width)
            down[some, columns] = dot_tn(grad[:, some], keep[:, columns]).astype(bf16)

        weight_gradients(
            ((first, weight, normal, first_out), (second, down, d_in, down_out)), 3
        )

    drain()


def hand_over(*refs):
    sources, norms, targets, (gain_out, shift_out) = refs[:4], refs[4], refs[5:9], refs[9:11]
    held, sems = refs[11:15], refs[15]
    has_down = lax.rem(lax.axis_index("section"), 2) == 1
    fetch = [pltpu.make_async_copy(sources[i], held[i], sems.at[0, i]) for i in range(4)]
    store = [pltpu.make_async_copy(held[i], targets[i], sems.at[1, i]) for i in range(4)]
    for i in range(3):
        fetch[i].start()

    @pl.when(has_down)
    def _():
        fetch[3].start()

    @pl.when(jnp.logical_not(has_down))
    def _():
        held[3][...] = jnp.zeros_like(held[3])
        store[3].start()

    width, own = norms.shape[1], gain_out.shape[1]
    turned = pltpu.roll(norms[...], lax.rem(width - lax.axis_index("dp") * own, width), 1)
    gain_out[...] = turned[0:1, :own]
    shift_out[...] = turned[1:2, :own]
    for i in range(3):
        fetch[i].wait()
        store[i].start()

    @pl.when(has_down)
    def _():
        fetch[3].wait()
        store[3].start()

    for i in range(4):
        store[i].wait()


def on_device(tokens, cotangent, segment_ids, first_weight, down_weight, ln_gain, ln_shift):
    sections = lax.axis_size("section")
    groups = lax.axis_size("dp")
    count, width = tokens.shape
    batches, length = segment_ids.shape
    hidden = first_weight.shape[2]
    units = hidden // width
    share = batches // sections
    levels = units if groups == 2 * units and (units + 1) // 2 * width <= count else 0
    columns_out = hidden // groups
    any_space = pl.BlockSpec(memory_space=pl.ANY)
    vmem = pl.BlockSpec(memory_space=pltpu.VMEM)
    dma = pltpu.SemaphoreType.DMA
    if levels:
        sums = [jax.ShapeDtypeStruct((1, width, columns_out), f32)] * 2
        sums.append(jax.ShapeDtypeStruct((8, width), f32))
    else:
        sums = [jax.ShapeDtypeStruct((width, hidden), bf16)] * 2
        sums.append(jax.ShapeDtypeStruct((2, width), f32))
    scratch = [
        pltpu.VMEM((count, width), bf16),
        pltpu.VMEM((count, hidden), bf16),
        pltpu.VMEM((count, hidden), bf16),
        pltpu.VMEM((count, width), bf16),
        pltpu.VMEM((count, width), bf16),
        pltpu.VMEM((count, 1), f32),
        pltpu.VMEM((count, width), bf16),
        pltpu.VMEM((count, width), bf16),
        pltpu.VMEM((width, hidden), bf16),
        pltpu.VMEM((width, hidden), bf16),
        pltpu.VMEM((2, 8, width), f32),
        pltpu.VMEM((width, length), f32),
        pltpu.VMEM((batches * 16, length), f32),
        pltpu.VMEM((batches, length), jnp.int32),
        pltpu.VMEM((2, 1, width), f32),
        dma((units + 4,)),
        dma((batches,)),
        dma((batches,)),
        dma((batches,)),
        dma((batches,)),
        dma((batches,)),
        dma((2, batches)),
        dma((2, share)),
        dma((2, units)),
    ]
    if levels:
        scratch += [
            pltpu.VMEM((width, columns_out), f32),
            pltpu.VMEM((2, levels + 1, width, columns_out), bf16),
            pltpu.VMEM((levels, 8, width), f32),
            pltpu.VMEM((2, 8, width), f32),
            pltpu.SemaphoreType.REGULAR((2,)),
            dma((2, 2, levels, HALVES)),
            dma((2, 2, levels + 1, HALVES)),
            dma((2, levels)),
        ]
    results = pl.pallas_call(
        functools.partial(pipeline, sections, levels),
        out_shape=(
            jax.ShapeDtypeStruct((count // sections, width), bf16),
            jax.ShapeDtypeStruct((count // sections, width), bf16),
            *sums,
        ),
        in_specs=[any_space] * 7,
        out_specs=(any_space, any_space, any_space, any_space, vmem),
        scratch_shapes=scratch,
        compiler_params=pltpu.CompilerParams(
            collective_id=0, has_side_effects=True, vmem_limit_bytes=64 * 2**20
        ),
    )(tokens, cotangent, segment_ids, first_weight, down_weight, ln_gain, ln_shift)
    if levels:
        own = jax.ShapeDtypeStruct((1, width // groups), f32)
        return pl.pallas_call(
            hand_over,
            out_shape=tuple(jax.ShapeDtypeStruct(r.shape, r.dtype) for r in results[:4]) + (own, own),
            in_specs=[any_space] * 4 + [vmem],
            out_specs=(any_space,) * 4 + (vmem,) * 2,
            scratch_shapes=[pltpu.VMEM(r.shape, r.dtype) for r in results[:4]] + [dma((2, 4))],
        )(*results)
    layer_rows, input_rows, first_sum, down_sum, norm_sum = results
    has_down = lax.rem(lax.axis_index("section"), 2) == 1
    down_sum = jnp.where(has_down, down_sum, jnp.zeros_like(down_sum))
    first_sum, down_sum, norm_sum = (
        lax.psum_scatter(value, "dp", scatter_dimension=1, tiled=True)
        for value in (first_sum, down_sum, norm_sum)
    )
    first_sum, down_sum = first_sum.astype(f32)[None], down_sum.astype(f32)[None]
    return (layer_rows, input_rows, first_sum, down_sum, norm_sum[0:1], norm_sum[1:2])


def solution(mesh):
    return jax.shard_map(
        on_device,
        mesh=mesh,
        in_specs=(
            P("dp", None),
            P("dp", None),
            P("dp", None),
            P("section", None, None),
            P("section", None, None),
            P("section", None),
            P("section", None),
        ),
        out_specs=(
            P(("dp", "section"), None),
            P(("dp", "section"), None),
            P("section", None, "dp"),
            P("section", None, "dp"),
            P("section", "dp"),
            P("section", "dp"),
        ),
        check_vma=False,
    )
```
